256 devices in a mesh: pop: 16 (over z, core), mp: 16 (over y, x).
Axes of the slice: x: 4, y: 4, z: 8, core: 2. Of those that a mesh axis runs over, the one named last changes fastest.
Arguments:
- tokens: bfloat16 [16384, 3584], P('pop', 'mp'), may hold values from -6 to 6
- target: bfloat16 [16384, 10240], P('pop', 'mp'), may hold values from -6 to 6
- unit_weight: float32 [10240], P('mp'), may hold values from 0.2 to 5
- gate_weight: bfloat16 [3584, 10240], P(None, 'mp'), may hold values from -0.09375 to 0.09375
- up_weight: bfloat16 [3584, 10240], P(None, 'mp'), may hold values from -0.09375 to 0.09375
- seeds: int32 [256], replicated, may hold values from 0 to 1073741823
Outputs:
- update_gate: float32 [3584, 10240], P('pop', 'mp')
- update_up: float32 [3584, 10240], P('pop', 'mp')
- fitness: float32 [512], P('pop')
The draws below stay inside these ranges and needn't reach their ends.
Inputs may be any that keep to these rules, and one draw needn't show every extreme that they name: seeds are independent integers, one for each antithetic pair.
All inputs are finite; a program needn't handle non-finite values.
Results may differ from the reference program's by a relative error of at most 0.0003.
Values may be sent and summed in bfloat16 or wider, within the bound.
No kernel may reach another device: no remote copies, remote signals or barrier semaphores. Data moves between devices by JAX's collectives and lax.ppermute only.
A program may use at most 128 MiB of HBM per device.

```python
import math
import jax
import jax.numpy as jnp
from jax import lax

D = 3584
FF = 10240
ROWS = 64
PAIRS = 256
TOKENS = 16384


def place_ends(array, key, least, largest):
    index_at = [jax.random.randint(jax.random.fold_in(key, axis), (), 0, length) for axis, length in enumerate(array.shape)]
    main_axis = array.shape.index(max(array.shape))
    next_to = index_at[:main_axis] + [(index_at[main_axis] + 1) % array.shape[main_axis]] + index_at[main_axis + 1:]
    return array.at[tuple(index_at)].set(least).at[tuple(next_to)].set(largest)


def block_levels(key, shape, shards, least, top_value):
    level = 1.0
    for dim, shards_of in shards:
        draws = jax.random.uniform(jax.random.fold_in(jax.random.fold_in(key, 6), dim), (shards_of,), jnp.float32, least / len(shards), top_value / len(shards))
        level = level * jnp.repeat(jnp.exp(draws), shape[dim] // shards_of).reshape((-1,) + (1,) * (len(shape) - 1 - dim))
    return level


def centred(key, dims, scale, bound, cuts=(), kind=jnp.bfloat16):
    drawn = jax.random.normal(key, dims, jnp.float32) * scale
    if len(cuts) > 0:
        drawn = block_levels(key, dims, cuts, -0.22, 0.18) * drawn
    return jnp.clip(drawn, min=-bound, max=bound).astype(kind)


def setup_inputs(seed: int = 0) -> dict:
    arg_keys = jax.random.split(jax.random.key(seed), 7)
    return {
        "tokens": centred(arg_keys[0], (TOKENS, D), 1.0, 6.0, ((0, 16), (1, 16))),
        "target": centred(arg_keys[1], (TOKENS, FF), 1.0, 6.0, ((0, 16), (1, 16))),
        "unit_weight": jnp.clip(jnp.exp(math.log(5.0) - 3.218876 * jax.random.uniform(arg_keys[2], (FF,), jnp.float32) ** block_levels(arg_keys[2], (FF,), ((0, 16),), -0.2, 0.2)), 0.2, 5.0),
        "gate_weight": centred(arg_keys[3], (D, FF), D ** -0.5, 0.09375, ((1, 16),)),
        "up_weight": centred(arg_keys[4], (D, FF), D ** -0.5, 0.09375, ((1, 16),)),
        "seeds": place_ends(jax.random.randint(arg_keys[5], (PAIRS,), 0, 1073741824), jax.random.fold_in(arg_keys[5], 1), 0, 1073741823).astype(jnp.int32),
    }


SIGMA = 0.5
EPSILON = 1e-05

def levels(seed_values, positions, columns, marker):
    mixed = seed_values * 747796405 + (positions * 4 + columns) * 277803737 + marker
    mixed = jnp.bitwise_xor(mixed, jnp.right_shift(mixed, 15))
    mixed = mixed * 1664525 + 1013904223
    mixed = jnp.bitwise_xor(mixed, jnp.right_shift(mixed, 13))
    return (2 * jnp.bitwise_and(mixed, 255) - 255).astype(jnp.float32) / 256.0

def reference(tokens, target, unit_weight, gate_weight, up_weight, seeds):
    scale = SIGMA / math.sqrt(D)
    rows_model = jnp.arange(D, dtype=jnp.int32)[:, None]
    rows_hidden = jnp.arange(FF, dtype=jnp.int32)[:, None]
    columns = jnp.arange(4, dtype=jnp.int32)[None, :]

    def one_pair(index):
        block = lax.dynamic_slice_in_dim(tokens, index * ROWS, ROWS, 0)
        goal = lax.dynamic_slice_in_dim(target, index * ROWS, ROWS, 0).astype(jnp.float32)
        seed_value = seeds[index]
        in_gate = levels(seed_value, rows_model, columns, 11003).astype(jnp.bfloat16)
        in_up = levels(seed_value, rows_model, columns, 33023).astype(jnp.bfloat16)
        gate_output = levels(seed_value, rows_hidden, columns, 22013)
        up_output = levels(seed_value, rows_hidden, columns, 44041)
        base_gate = jnp.dot(block, gate_weight, preferred_element_type=jnp.float32)
        base_up = jnp.dot(block, up_weight, preferred_element_type=jnp.float32)
        low_gate = jnp.dot(block, in_gate, preferred_element_type=jnp.float32)
        low_up = jnp.dot(block, in_up, preferred_element_type=jnp.float32)
        side_gate = jnp.dot(low_gate, gate_output.T, precision=lax.Precision.HIGHEST) * scale
        side_up = jnp.dot(low_up, up_output.T, precision=lax.Precision.HIGHEST) * scale
        results = []
        for sign in (1.0, -1.0):
            hidden = jax.nn.silu(base_gate + sign * side_gate) * (base_up + sign * side_up)
            results.append(jnp.sum(unit_weight * (hidden - goal) ** 2))
        return jnp.stack(results) / (ROWS * FF)
    errors = lax.map(one_pair, jnp.arange(PAIRS, dtype=jnp.int32))
    scores = -errors.reshape(-1)
    center = jnp.mean(scores)
    spread = jnp.mean((scores - center) ** 2)
    fitness = (scores - center) / jnp.sqrt(spread + EPSILON)
    pair_weight = (fitness[0::2] - fitness[1::2]) / 2.0
    factor = (pair_weight / math.sqrt(PAIRS))[None, :, None]
    all_seeds = seeds[None, :, None]
    model_index = jnp.arange(D, dtype=jnp.int32)[:, None, None]
    hidden_index = jnp.arange(FF, dtype=jnp.int32)[:, None, None]
    corner = jnp.arange(4, dtype=jnp.int32)[None, None, :]
    updates = []
    for first, second in ((11003, 22013), (33023, 44041)):
        left = (levels(all_seeds, model_index, corner, first) * factor).reshape(D, PAIRS * 4)
        right = levels(all_seeds, hidden_index, corner, second).reshape(FF, PAIRS * 4)
        updates.append(jnp.dot(left, right.T, precision=lax.Precision.HIGHEST))
    return (updates[0], updates[1], fitness)
```

```python
import math

import jax
import jax.numpy as jnp
from jax import lax
from jax.experimental import pallas as pl
from jax.experimental.pallas import tpu as pltpu
from jax.sharding import PartitionSpec as P

FF = 10240
ROWS = 64
SIGMA = 0.5
EPSILON = 1e-05
SEED_STEP = 747796405
CELL_STEP = 277803737
VMEM = 48 * 1024 * 1024

WAYS = {"+x": (1, 0), "-x": (3, 0), "+y": (0, 1), "-y": (0, 3)}
STEPS = (
    (((0, 0), "+x"), ((0, 0), "-x"), ((0, 0), "+y"), ((0, 0), "-y")),
    (((0, 1), "+x"), ((0, 3), "-x"), ((3, 0), "+y"), ((1, 0), "-y")),
    (((1, 0), "+x"), ((3, 1), "-x"), ((0, 1), "+y"), ((3, 3), "-y")),
    (((1, 3), "+x"), ((1, 1), "+y"), ((3, 2), "-x")),
)


def moved(place, way):
    return ((place[0] + WAYS[way][0]) % 4, (place[1] + WAYS[way][1]) % 4)


def pairs_of(way):
    dx, dy = WAYS[way]
    return [(y * 4 + x, (y + dy) % 4 * 4 + (x + dx) % 4) for y in range(4) for x in range(4)]


def source_of(place):
    me = lax.axis_index("mp")
    return lax.rem(me // 4 + 4 - place[1], 4) * 4 + lax.rem(lax.rem(me, 4) + 4 - place[0], 4)


def levels_of(mixed):
    mixed = jnp.bitwise_xor(mixed, jnp.right_shift(mixed, 15))
    mixed = mixed * 1664525 + 1013904223
    mixed = jnp.bitwise_xor(mixed, jnp.right_shift(mixed, 13))
    level = (2 * jnp.bitwise_and(mixed, 255) - 255).astype(jnp.float32) * (1.0 / 256.0)
    return level.astype(jnp.bfloat16)


def iota(shape, dim):
    return lax.broadcasted_iota(jnp.int32, shape, dim)


def in_table_kernel(lane_ref, out_ref):
    rows = 64

    @pl.loop(0, out_ref.shape[0] // rows)
    def _(i):
        at = pl.multiple_of(i * rows, rows)
        cell = (iota((rows, 128), 0) + at) * (4 * CELL_STEP)
        out_ref[pl.ds(at, rows), :] = levels_of(lane_ref[...] + cell)


def out_table_kernel(column_ref, gate_ref, up_ref, right_gate_ref, right_up_ref):
    width = right_gate_ref.shape[1]
    first = lax.axis_index("mp") * width
    rows = 16
    cell = (iota((rows, width), 1) + first) * (4 * CELL_STEP)

    @pl.loop(0, right_gate_ref.shape[0] // rows)
    def _(i):
        at = pl.multiple_of(i * rows, rows)
        right_gate_ref[pl.ds(at, rows), :] = levels_of(column_ref[pl.ds(at, rows), 0:1] + cell)
        right_up_ref[pl.ds(at, rows), :] = levels_of(column_ref[pl.ds(at, rows), 1:2] + cell)

    mine = lax.axis_index("pop") * 64
    for half in (0, 128):
        gate_ref[half + 0 : half + 64, :] = right_gate_ref[pl.ds(mine, 64), :]
        gate_ref[half + 64 : half + 128, :] = jnp.zeros((64, width), jnp.bfloat16)
        up_ref[half + 0 : half + 64, :] = jnp.zeros((64, width), jnp.bfloat16)
        up_ref[half + 64 : half + 128, :] = right_up_ref[pl.ds(mine, 64), :]


def left_table_kernel(lane_ref, left_gate_ref, left_up_ref):
    rows = 16
    count, width = left_gate_ref.shape
    first = lax.axis_index("pop") * count

    @pl.loop(0, count // rows)
    def _(i):
        at = pl.multiple_of(i * rows, rows)
        cell = (iota((rows, width), 0) + (at + first)) * (4 * CELL_STEP)
        left_gate_ref[pl.ds(at, rows), :] = levels_of(lane_ref[0:1, :] + cell)
        left_up_ref[pl.ds(at, rows), :] = levels_of(lane_ref[1:2, :] + cell)


def contract(a, b):
    return lax.dot_general(a, b, (((0,), (0,)), ((), ())), preferred_element_type=jnp.float32)


def block_copies(places, blocks, gate_ref, up_ref, table_ref, x_ref, w_ref, sems):
    depth = blocks[0].shape[0]
    width = gate_ref.shape[1]
    copies = []
    for i, (place, block) in enumerate(zip(places, blocks)):
        rows = pl.ds(source_of(place) * depth, depth)
        mine = pl.ds(i * depth, depth)
        copies.append(
            [
                pltpu.make_async_copy(block, x_ref.at[mine, :], sems.at[4 * i]),
                pltpu.make_async_copy(gate_ref.at[rows, :], w_ref.at[mine, pl.ds(0, width)], sems.at[4 * i + 1]),
                pltpu.make_async_copy(up_ref.at[rows, :], w_ref.at[mine, pl.ds(width, width)], sems.at[4 * i + 2]),
                pltpu.make_async_copy(table_ref.at[rows, :], w_ref.at[mine, pl.ds(2 * width, 128)], sems.at[4 * i + 3]),
            ]
        )
    return copies


def first_kernel(places, slabs, *refs):
    n = len(places)
    blocks, (gate_ref, up_ref, table_ref, acc_ref, x_ref, w_ref, sems) = refs[:n], refs[n:]
    depth = blocks[0].shape[0]
    copies = block_copies(places, blocks, gate_ref, up_ref, table_ref, x_ref, w_ref, sems)
    for group in copies:
        for copy in group:
            copy.start()
    done = 0
    for slab in slabs:
        for group in copies[done : done + slab]:
            for copy in group:
                copy.wait()
        low, high = done * depth, (done + slab) * depth

        @pl.loop(0, acc_ref.shape[0] // 256)
        def _(i):
            rows = pl.ds(pl.multiple_of(i * 256, 256), 256)
            part = contract(x_ref[low:high, rows], w_ref[low:high, :])
            if low == 0:
                acc_ref[rows, :] = part
            else:
                acc_ref[rows, :] += part

        done += slab


def last_kernel(places, *refs):
    n = len(places)
    blocks = refs[:n]
    gate_ref, up_ref, table_ref, acc_ref, target_ref, weight_ref, gate_out_ref, up_out_ref = refs[n : n + 8]
    message_ref, x_ref, w_ref, a_ref, t_ref, total_ref, side_ref, parts_ref, sems, a_sems, t_sems = refs[n + 8 :]
    width = gate_ref.shape[1]
    tile = 256
    tiles = acc_ref.shape[0] // tile
    copies = block_copies(places, blocks, gate_ref, up_ref, table_ref, x_ref, w_ref, sems)
    for group in copies:
        for copy in group:
            copy.start()
    for i in range(tiles):
        rows = pl.ds(i * tile, tile)
        pltpu.make_async_copy(acc_ref.at[rows, :], a_ref.at[rows, :], a_sems.at[i]).start()
        pltpu.make_async_copy(target_ref.at[rows, :], t_ref.at[rows, :], t_sems.at[i]).start()
    for group in copies:
        for copy in group:
            copy.wait()
    scale = SIGMA / math.sqrt(16 * blocks[0].shape[0])
    lane_pair = lax.rem(iota((tile, 128), 1), 64) // 4
    row_pair = iota((tile, 128), 0) // ROWS

    @pl.loop(0, tiles)
    def _(i):
        rows = pl.ds(pl.multiple_of(i * tile, tile), tile)
        pltpu.make_async_copy(acc_ref.at[rows, :], a_ref.at[rows, :], a_sems.at[i]).wait()
        pltpu.make_async_copy(target_ref.at[rows, :], t_ref.at[rows, :], t_sems.at[i]).wait()
        part = contract(x_ref[:, rows], w_ref[...]) + a_ref[rows, :]
        total_ref[...] = part[:, : 2 * width]
        low = jnp.where(lane_pair == row_pair + i * (tile // ROWS), part[:, 2 * width :] * scale, 0.0)
        high = low.astype(jnp.bfloat16)
        rest = (low - high.astype(jnp.float32)).astype(jnp.bfloat16)
        low_both = jnp.concatenate([high, rest], axis=1)
        side_ref[:, :width] = jnp.dot(low_both, gate_out_ref[...], preferred_element_type=jnp.float32)
        side_ref[:, width:] = jnp.dot(low_both, up_out_ref[...], preferred_element_type=jnp.float32)

        @pl.loop(0, tile // ROWS)
        def _(p):
            plus = jnp.zeros((8, width), jnp.float32)
            minus = jnp.zeros((8, width), jnp.float32)
            for q in range(ROWS // 16):
                at16 = pl.multiple_of(p * ROWS + q * 16, 16)
                goals = t_ref[pl.ds(pl.multiple_of(i * tile + at16, 16), 16), :].astype(jnp.float32)
                for h in range(2):
                    here = pl.ds(pl.multiple_of(at16 + h * 8, 8), 8)
                    goal = goals[h * 8 : h * 8 + 8, :]
                    gate, up = total_ref[here, :width], total_ref[here, width:]
                    side_gate, side_up = side_ref[here, :width], side_ref[here, width:]
                    half = 0.5 * (gate + side_gate)
                    error = (half * jnp.tanh(half) + half) * (up + side_up) - goal
                    plus += error * error
                    half = 0.5 * (gate - side_gate)
                    error = (half * jnp.tanh(half) + half) * (up - side_up) - goal
                    minus += error * error
            k = i * (tile // ROWS) + p
            parts_ref[0, pl.ds(k, 1), :] = jnp.sum(plus, axis=0, keepdims=True) * weight_ref[...]
            parts_ref[1, pl.ds(k, 1), :] = jnp.sum(minus, axis=0, keepdims=True) * weight_ref[...]

    odd = lax.rem(lax.axis_index("pop"), 2)
    pairs = parts_ref.shape[1]
    lane = iota((pairs, 128), 1)
    keep = lane // 4 == iota((pairs, 128), 0) + odd * 16
    lines = []
    for s in range(2):
        sums = jnp.sum(parts_ref[s], axis=1, keepdims=True) * (1.0 / (ROWS * FF))
        lines.append(jnp.sum(jnp.where(keep, sums, 0.0), axis=0, keepdims=True))
    row = iota((8, 128), 0)
    both = jnp.where(lax.rem(row, 2) == 0, lines[0], lines[1])

    @pl.loop(0, message_ref.shape[0] // 8)
    def _(i):
        message_ref[pl.ds(pl.multiple_of(i * 8, 8), 8), :] = both


def update_kernel(message_ref, left_gate_ref, left_up_ref, right_gate_ref, right_up_ref, out_gate_ref, out_up_ref, fit_ref, f_ref):
    count = message_ref.shape[0]
    pick_row, pick = iota((16, count), 0), iota((16, count), 1)
    chosen = (pick // 64 == lax.rem(pick_row, 8)) & (lax.rem(pick, 2) == pick_row // 8)
    summed = jnp.dot(
        chosen.astype(jnp.float32),
        message_ref[...],
        precision=lax.Precision.HIGHEST,
        preferred_element_type=jnp.float32,
    )
    scores = -summed
    members = 4.0 * 512.0
    center = jnp.sum(scores) / members
    spread = jnp.sum((scores - center) ** 2) / members
    fitness = (scores - center) / jnp.sqrt(jnp.full((16, 128), spread + EPSILON, jnp.float32))
    f_ref[...] = fitness
    factor = (fitness[:8] - fitness[8:]) * (0.5 / 16.0)
    for left_ref, right_ref, out_ref in (
        (left_gate_ref, right_gate_ref, out_gate_ref),
        (left_up_ref, right_up_ref, out_up_ref),
    ):
        highs, rests = [], []
        for q in range(8):
            scaled = left_ref[:, q * 128 : (q + 1) * 128].astype(jnp.float32) * factor[q : q + 1, :]
            high = scaled.astype(jnp.bfloat16)
            highs.append(high)
            rests.append((scaled - high.astype(jnp.float32)).astype(jnp.bfloat16))
        out_ref[...] = jnp.dot(
            jnp.concatenate(highs, axis=1), right_ref[...], preferred_element_type=jnp.float32
        ) + jnp.dot(jnp.concatenate(rests, axis=1), right_ref[...], preferred_element_type=jnp.float32)
    pop = lax.axis_index("pop")
    mine = pop // 2
    lane, member = iota((128, 128), 0), iota((128, 128), 1)
    at = lane == lax.rem(pop, 2) * 64 + member // 2 * 4
    total = jnp.zeros((1, 128), jnp.float32)
    for s in range(2):
        line = jnp.broadcast_to(f_ref[pl.ds(mine + 8 * s, 1), :], (8, 128))
        select = (at & (lax.rem(member, 2) == s)).astype(jnp.float32)
        total += jnp.dot(line, select, precision=lax.Precision.HIGHEST, preferred_element_type=jnp.float32)[:1]
    fit_ref[...] = total[:, : fit_ref.shape[1]]


def params():
    return pltpu.CompilerParams(vmem_limit_bytes=VMEM)


def cost(flops, size):
    return pl.CostEstimate(flops=flops, bytes_accessed=size, transcendentals=0)


def on_device(tokens, target, unit_weight, gate_weight, up_weight, seeds):
    rows_dev, depth = tokens.shape
    model_width, width = gate_weight.shape
    pairs_dev = rows_dev // ROWS
    pair_total = seeds.shape[0]
    device_total = lax.axis_size("pop") * lax.axis_size("mp")
    any_space = pl.BlockSpec(memory_space=pl.ANY)
    in_vmem = pl.BlockSpec(memory_space=pltpu.VMEM)

    mine = tokens.T
    blocks = {(0, 0): mine}
    for step in STEPS:
        for place, way in step:
            blocks[moved(place, way)] = lax.ppermute(blocks[place], "mp", pairs_of(way))
    late = [moved(place, way) for place, way in STEPS[-1]]
    early = [place for place in blocks if place not in late]

    corner = jnp.tile(jnp.arange(4, dtype=jnp.int32) * CELL_STEP, pair_total)
    by_lane = jnp.repeat(seeds * SEED_STEP, 4) + corner
    local_lane = lax.dynamic_slice_in_dim(by_lane, lax.axis_index("pop") * pairs_dev * 4, pairs_dev * 4)
    in_lanes = jnp.concatenate([local_lane + 11003, local_lane + 33023])[None, :]
    left_lanes = jnp.stack([by_lane + 11003, by_lane + 33023])
    out_columns = jnp.stack([by_lane + 22013, by_lane + 44041], axis=1)

    bf16 = jnp.bfloat16
    table = pl.pallas_call(
        in_table_kernel,
        out_shape=jax.ShapeDtypeStruct((model_width, 128), bf16),
        in_specs=[in_vmem],
        out_specs=in_vmem,
        compiler_params=params(),
        cost_estimate=cost(2_000_000_000, 1_000_000),
        name="in_table",
    )(in_lanes)
    gate_out, up_out, right_gate, right_up = pl.pallas_call(
        out_table_kernel,
        out_shape=[jax.ShapeDtypeStruct((256, width), bf16)] * 2 + [jax.ShapeDtypeStruct((pair_total * 4, width), bf16)] * 2,
        in_specs=[in_vmem],
        out_specs=[in_vmem] * 4,
        compiler_params=params(),
        cost_estimate=cost(4_000_000_000, 3_000_000),
        name="out_table",
    )(out_columns)
    left_rows = model_width // lax.axis_size("pop")
    left_gate, left_up = pl.pallas_call(
        left_table_kernel,
        out_shape=[jax.ShapeDtypeStruct((left_rows, pair_total * 4), bf16)] * 2,
        in_specs=[in_vmem],
        out_specs=[in_vmem] * 2,
        compiler_params=params(),
        cost_estimate=cost(2_000_000_000, 1_000_000),
        name="left_table",
    )(left_lanes)

    columns = 2 * width + 128
    n = len(early)
    acc = pl.pallas_call(
        lambda *refs: first_kernel(early, (8, n - 8), *refs),
        out_shape=jax.ShapeDtypeStruct((rows_dev, columns), jnp.float32),
        in_specs=[any_space] * (n + 3),
        out_specs=in_vmem,
        scratch_shapes=[
            pltpu.VMEM((n * depth, rows_dev), bf16),
            pltpu.VMEM((n * depth, columns), bf16),
            pltpu.SemaphoreType.DMA((4 * n,)),
        ],
        compiler_params=params(),
        cost_estimate=cost(2 * rows_dev * n * depth * columns, 20_000_000),
        name="first_blocks",
    )(*[blocks[place] for place in early], gate_weight, up_weight, table)

    n = len(late)
    message = pl.pallas_call(
        lambda *refs: last_kernel(late, *refs),
        out_shape=jax.ShapeDtypeStruct((2 * device_total, 128), jnp.float32),
        in_specs=[any_space] * (n + 5) + [in_vmem] * 3,
        out_specs=in_vmem,
        scratch_shapes=[
            pltpu.VMEM((n * depth, rows_dev), bf16),
            pltpu.VMEM((n * depth, columns), bf16),
            pltpu.VMEM((rows_dev, columns), jnp.float32),
            pltpu.VMEM((rows_dev, width), bf16),
            pltpu.VMEM((256, 2 * width), jnp.float32),
            pltpu.VMEM((256, 2 * width), jnp.float32),
            pltpu.VMEM((2, pairs_dev, width), jnp.float32),
            pltpu.SemaphoreType.DMA((4 * n,)),
            pltpu.SemaphoreType.DMA((rows_dev // 256,)),
            pltpu.SemaphoreType.DMA((rows_dev // 256,)),
        ],
        compiler_params=params(),
        cost_estimate=cost(2 * rows_dev * n * depth * columns, 12_000_000),
        name="last_blocks",
    )(*[blocks[place] for place in late], gate_weight, up_weight, table, acc, target, unit_weight[None, :], gate_out, up_out)

    received = lax.all_to_all(message, ("pop", "mp"), 0, 0, tiled=True)

    update_gate, update_up, fitness = pl.pallas_call(
        update_kernel,
        out_shape=[jax.ShapeDtypeStruct((left_rows, width), jnp.float32)] * 2
        + [jax.ShapeDtypeStruct((1, 2 * pairs_dev), jnp.float32)],
        in_specs=[in_vmem] * 5,
        out_specs=[in_vmem] * 3,
        scratch_shapes=[pltpu.VMEM((16, 128), jnp.float32)],
        compiler_params=params(),
        cost_estimate=cost(1_200_000_000, 5_000_000),
        name="update",
    )(received, left_gate, left_up, right_gate, right_up)
    return (update_gate, update_up, fitness.reshape(2 * pairs_dev))


def solution(mesh):
    return jax.shard_map(
        on_device,
        mesh=mesh,
        in_specs=(P("pop", "mp"), P("pop", "mp"), P("mp"), P(None, "mp"), P(None, "mp"), P()),
        out_specs=(P("pop", "mp"), P("pop", "mp"), P("pop")),
        check_vma=False,
    )
```

```python
import math

import jax
import jax.numpy as jnp
from jax import lax
from jax.experimental import pallas as pl
from jax.experimental.pallas import tpu as pltpu
from jax.sharding import PartitionSpec as P

FF = 10240
ROWS = 64
SIGMA = 0.5
EPSILON = 1e-05
SEED_STEP = 747796405
CELL_STEP = 277803737

WAYS = {"+x": (1, 0), "-x": (3, 0), "+y": (0, 1), "-y": (0, 3)}
ROUNDS = (
    (((0, 0), "+x"), ((0, 0), "-y"), ((0, 0), "-x"), ((0, 0), "+y")),
    (((1, 0), "+x"), ((0, 3), "-y"), ((0, 3), "-x"), ((1, 0), "+y")),
    (((0, 3), "+x"), ((2, 0), "-y"), ((0, 1), "-x"), ((2, 0), "+y")),
    (((0, 2), "+x"), ((0, 2), "-x"), ((2, 3), "-y")),
)


def moved(place, way):
    return ((place[0] + WAYS[way][0]) % 4, (place[1] + WAYS[way][1]) % 4)


def pairs_of(way):
    dx, dy = WAYS[way]
    return [(y * 4 + x, (y + dy) % 4 * 4 + (x + dx) % 4) for y in range(4) for x in range(4)]


def source_of(place):
    me = lax.axis_index("mp")
    return lax.rem(me // 4 + 4 - place[1], 4) * 4 + lax.rem(lax.rem(me, 4) + 4 - place[0], 4)


def levels_of(mixed):
    mixed = jnp.bitwise_xor(mixed, jnp.right_shift(mixed, 15))
    mixed = mixed * 1664525 + 1013904223
    mixed = jnp.bitwise_xor(mixed, jnp.right_shift(mixed, 13))
    level = jnp.bitwise_and(mixed, 255).astype(jnp.float32) * (2.0 / 256.0) - 255.0 / 256.0
    return level.astype(jnp.bfloat16)


def iota(shape, dim):
    return lax.broadcasted_iota(jnp.int32, shape, dim)


def in_table_kernel(lane_ref, out_ref):
    rows = 64

    @pl.loop(0, out_ref.shape[0] // rows)
    def _(i):
        at = pl.multiple_of(i * rows, rows)
        cell = (iota((rows, 128), 0) + at) * (4 * CELL_STEP)
        out_ref[pl.ds(at, rows), :] = levels_of(lane_ref[...] + cell)


def side_table_kernel(column_ref, gate_ref, up_ref):
    width = gate_ref.shape[1]
    first = lax.axis_index("mp") * width
    cell = (iota((16, width), 1) + first) * (4 * CELL_STEP)
    nothing = jnp.zeros((64, width), jnp.bfloat16)
    for i in range(4):
        gate = levels_of(column_ref[i * 16 : i * 16 + 16, :] + cell)
        up = levels_of(column_ref[64 + i * 16 : 64 + i * 16 + 16, :] + cell)
        for half in (0, 128):
            gate_ref[half + i * 16 : half + i * 16 + 16, :] = gate
            up_ref[half + 64 + i * 16 : half + 64 + i * 16 + 16, :] = up
    for half in (0, 128):
        gate_ref[half + 64 : half + 128, :] = nothing
        up_ref[half : half + 64, :] = nothing


def factor_kernel(column_ref, lane_ref, left_gate_ref, left_up_ref, right_gate_ref, right_up_ref):
    width = right_gate_ref.shape[1]
    first = lax.axis_index("mp") * width
    rows = 16
    cell = (iota((rows, width), 1) + first) * (4 * CELL_STEP)

    @pl.loop(0, right_gate_ref.shape[0] // rows)
    def _(i):
        at = pl.multiple_of(i * rows, rows)
        right_gate_ref[pl.ds(at, rows), :] = levels_of(column_ref[pl.ds(at, rows), 0:1] + cell)
        right_up_ref[pl.ds(at, rows), :] = levels_of(column_ref[pl.ds(at, rows), 1:2] + cell)

    count, across = left_gate_ref.shape
    left_first = lax.axis_index("pop") * count

    @pl.loop(0, count // rows)
    def _(i):
        at = pl.multiple_of(i * rows, rows)
        step = (iota((rows, across), 0) + (at + left_first)) * (4 * CELL_STEP)
        left_gate_ref[pl.ds(at, rows), :] = levels_of(lane_ref[0:1, :] + step)
        left_up_ref[pl.ds(at, rows), :] = levels_of(lane_ref[1:2, :] + step)


def contract(a, b):
    return lax.dot_general(a, b, (((0,), (0,)), ((), ())), preferred_element_type=jnp.float32)


def block_copies(places, blocks, gate_ref, up_ref, table_ref, x_ref, w_ref, sems):
    depth = blocks[0].shape[0]
    width = gate_ref.shape[1]
    copies = []
    for i, (place, block) in enumerate(zip(places, blocks)):
        rows = pl.ds(source_of(place) * depth, depth)
        mine = pl.ds(i * depth, depth)
        copies.append(
            [
                pltpu.make_async_copy(block, x_ref.at[mine, :], sems.at[4 * i]),
                pltpu.make_async_copy(gate_ref.at[rows, :], w_ref.at[mine, pl.ds(0, width)], sems.at[4 * i + 1]),
                pltpu.make_async_copy(up_ref.at[rows, :], w_ref.at[mine, pl.ds(width, width)], sems.at[4 * i + 2]),
                pltpu.make_async_copy(table_ref.at[rows, :], w_ref.at[mine, pl.ds(2 * width, 128)], sems.at[4 * i + 3]),
            ]
        )
    return copies


def round_kernel(places, fresh, *refs):
    n = len(places)
    blocks, rest = refs[:n], refs[n:]
    gate_ref, up_ref, table_ref = rest[:3]
    acc_ref, x_ref, w_ref, sems = rest[-4:]
    copies = block_copies(places, blocks, gate_ref, up_ref, table_ref, x_ref, w_ref, sems)
    for group in copies:
        for copy in group:
            copy.start()
    for group in copies:
        for copy in group:
            copy.wait()

    @pl.loop(0, acc_ref.shape[0] // 256)
    def _(i):
        rows = pl.ds(pl.multiple_of(i * 256, 256), 256)
        part = contract(x_ref[:, rows], w_ref[...])
        if fresh:
            acc_ref[rows, :] = part
        else:
            acc_ref[rows, :] = rest[3][rows, :] + part


def last_kernel(places, *refs):
    n = len(places)
    blocks = refs[:n]
    gate_ref, up_ref, table_ref, acc_ref, target_ref, weight_ref, gate_out_ref, up_out_ref = refs[n : n + 8]
    message_ref, x_ref, w_ref, t_ref, total_ref, side_ref, parts_ref, sems, t_sems = refs[n + 8 :]
    width = gate_ref.shape[1]
    tile = 256
    tiles = acc_ref.shape[0] // tile
    copies = block_copies(places, blocks, gate_ref, up_ref, table_ref, x_ref, w_ref, sems)
    for group in copies:
        for copy in group:
            copy.start()
    for i in range(tiles):
        rows = pl.ds(i * tile, tile)
        pltpu.make_async_copy(target_ref.at[rows, :], t_ref.at[rows, :], t_sems.at[i]).start()
    for group in copies:
        for copy in group:
            copy.wait()
    scale = SIGMA / math.sqrt(16 * blocks[0].shape[0])
    lane_pair = lax.rem(iota((tile, 128), 1), 64) // 4
    row_pair = iota((tile, 128), 0) // ROWS

    @pl.loop(0, tiles)
    def _(i):
        rows = pl.ds(pl.multiple_of(i * tile, tile), tile)
        pltpu.make_async_copy(target_ref.at[rows, :], t_ref.at[rows, :], t_sems.at[i]).wait()
        part = contract(x_ref[:, rows], w_ref[...]) + acc_ref[rows, :]
        total_ref[...] = part[:, : 2 * width]
        low = jnp.where(lane_pair == row_pair + i * (tile // ROWS), part[:, 2 * width :] * scale, 0.0)
        high = low.astype(jnp.bfloat16)
        rest = (low - high.astype(jnp.float32)).astype(jnp.bfloat16)
        low_both = jnp.concatenate([high, rest], axis=1)
        side_ref[:, :width] = jnp.dot(low_both, gate_out_ref[...], preferred_element_type=jnp.float32)
        side_ref[:, width:] = jnp.dot(low_both, up_out_ref[...], preferred_element_type=jnp.float32)

        @pl.loop(0, tile // ROWS)
        def _(p):
            plus = jnp.zeros((8, width), jnp.float32)
            minus = jnp.zeros((8, width), jnp.float32)
            for q in range(ROWS // 16):
                at16 = pl.multiple_of(p * ROWS + q * 16, 16)
                goals = t_ref[pl.ds(pl.multiple_of(i * tile + at16, 16), 16), :].astype(jnp.float32)
                for h in range(2):
                    here = pl.ds(pl.multiple_of(at16 + h * 8, 8), 8)
                    goal = goals[h * 8 : h * 8 + 8, :]
                    gate, up = total_ref[here, :width], total_ref[here, width:]
                    side_gate, side_up = side_ref[here, :width], side_ref[here, width:]
                    half = 0.5 * (gate + side_gate)
                    error = (half * jnp.tanh(half) + half) * (up + side_up) - goal
                    plus += error * error
                    half = 0.5 * (gate - side_gate)
                    error = (half * jnp.tanh(half) + half) * (up - side_up) - goal
                    minus += error * error
            k = i * (tile // ROWS) + p
            parts_ref[0, pl.ds(k, 1), :] = jnp.sum(plus, axis=0, keepdims=True) * weight_ref[...]
            parts_ref[1, pl.ds(k, 1), :] = jnp.sum(minus, axis=0, keepdims=True) * weight_ref[...]

    pairs = parts_ref.shape[1]
    lane = iota((pairs, 128), 1)
    pair = iota((pairs, 128), 0)
    line = jnp.zeros((1, 128), jnp.float32)
    for s in range(2):
        sums = jnp.sum(parts_ref[s], axis=1, keepdims=True) * (1.0 / (ROWS * FF))
        line += jnp.sum(jnp.where(lane // 4 == pair + 16 * s, sums, 0.0), axis=0, keepdims=True)
    message_ref[...] = jnp.broadcast_to(line, message_ref.shape)


def update_kernel(message_ref, left_gate_ref, left_up_ref, right_gate, right_up, *refs):
    out_gate_ref, out_up_ref, fit_ref, f_ref, right_gate_ref, right_up_ref, sems = refs
    gate_copy = pltpu.make_async_copy(right_gate, right_gate_ref, sems.at[0])
    up_copy = pltpu.make_async_copy(right_up, right_up_ref, sems.at[1])
    gate_copy.start()
    up_copy.start()
    count = message_ref.shape[0]
    pick_row, pick = iota((16, count), 0), iota((16, count), 1)
    chosen = pick // 16 == 2 * lax.rem(pick_row, 8) + pick_row // 8
    by_pop = jnp.dot(
        chosen.astype(jnp.float32),
        message_ref[...],
        precision=lax.Precision.HIGHEST,
        preferred_element_type=jnp.float32,
    )
    even, odd = by_pop[:8], by_pop[8:]
    low_lane = iota((8, 128), 1) < 64
    plus = jnp.where(low_lane, even, pltpu.roll(odd, 64, 1))
    minus = jnp.where(low_lane, pltpu.roll(even, 64, 1), odd)
    summed = jnp.concatenate([plus, minus], axis=0)
    scores = -summed
    members = 4.0 * 512.0
    center = jnp.sum(scores) / members
    spread = jnp.sum((scores - center) ** 2) / members
    fitness = (scores - center) / jnp.sqrt(jnp.full((16, 128), spread + EPSILON, jnp.float32))
    f_ref[...] = fitness
    factor = (fitness[:8] - fitness[8:]) * (0.5 / 16.0)
    for left_ref, right_ref, copy, out_ref in (
        (left_gate_ref, right_gate_ref, gate_copy, out_gate_ref),
        (left_up_ref, right_up_ref, up_copy, out_up_ref),
    ):
        highs, rests = [], []
        for q in range(8):
            scaled = left_ref[:, q * 128 : (q + 1) * 128].astype(jnp.float32) * factor[q : q + 1, :]
            high = scaled.astype(jnp.bfloat16)
            highs.append(high)
            rests.append((scaled - high.astype(jnp.float32)).astype(jnp.bfloat16))
        copy.wait()
        out_ref[...] = jnp.dot(
            jnp.concatenate(highs, axis=1), right_ref[...], preferred_element_type=jnp.float32
        ) + jnp.dot(jnp.concatenate(rests, axis=1), right_ref[...], preferred_element_type=jnp.float32)
    pop = lax.axis_index("pop")
    mine = pop // 2
    lane, member = iota((128, 128), 0), iota((128, 128), 1)
    at = lane == lax.rem(pop, 2) * 64 + member // 2 * 4
    total = jnp.zeros((1, 128), jnp.float32)
    for s in range(2):
        line = jnp.broadcast_to(f_ref[pl.ds(mine + 8 * s, 1), :], (8, 128))
        select = (at & (lax.rem(member, 2) == s)).astype(jnp.float32)
        total += jnp.dot(line, select, precision=lax.Precision.HIGHEST, preferred_element_type=jnp.float32)[:1]
    fit_ref[...] = total[:, : fit_ref.shape[1]]


def params(mib):
    return pltpu.CompilerParams(vmem_limit_bytes=mib * 1024 * 1024)


def cost(flops, size):
    return pl.CostEstimate(flops=flops, bytes_accessed=size, transcendentals=0)


def after(value, *others):
    return lax.optimization_barrier((value, *others))[0]


def on_device(tokens, target, unit_weight, gate_weight, up_weight, seeds):
    rows_dev, depth = tokens.shape
    model_width, width = gate_weight.shape
    pairs_dev = rows_dev // ROWS
    pair_total = seeds.shape[0]
    device_total = lax.axis_size("pop") * lax.axis_size("mp")
    any_space = pl.BlockSpec(memory_space=pl.ANY)
    in_vmem = pl.BlockSpec(memory_space=pltpu.VMEM)
    bf16, f32 = jnp.bfloat16, jnp.float32

    corner = jnp.tile(jnp.arange(4, dtype=jnp.int32) * CELL_STEP, pair_total)
    by_lane = jnp.repeat(seeds * SEED_STEP, 4) + corner
    local_lane = lax.dynamic_slice_in_dim(by_lane, lax.axis_index("pop") * pairs_dev * 4, pairs_dev * 4)
    in_lanes = jnp.concatenate([local_lane + 11003, local_lane + 33023])[None, :]
    side_columns = jnp.concatenate([local_lane + 22013, local_lane + 44041])[:, None]

    left_lanes = jnp.stack([by_lane + 11003, by_lane + 33023])
    right_columns = jnp.stack([by_lane + 22013, by_lane + 44041], axis=1)

    table = pl.pallas_call(
        in_table_kernel,
        out_shape=jax.ShapeDtypeStruct((model_width, 128), bf16),
        in_specs=[in_vmem],
        out_specs=in_vmem,
        compiler_params=params(4),
        cost_estimate=cost(1_000_000_000, 1_000_000),
        name="in_table",
    )(in_lanes)
    gate_out, up_out = pl.pallas_call(
        side_table_kernel,
        out_shape=[jax.ShapeDtypeStruct((256, width), bf16)] * 2,
        in_specs=[in_vmem],
        out_specs=[in_vmem] * 2,
        compiler_params=params(4),
        cost_estimate=cost(500_000_000, 300_000),
        name="side_table",
    )(side_columns)

    columns = 2 * width + 128

    def multiply(places, acc):
        n = len(places)
        given = [blocks[place] for place in places] + [gate_weight, up_weight, table]
        specs = [any_space] * (n + 3)
        if acc is not None:
            given.append(acc)
            specs.append(in_vmem)
        return pl.pallas_call(
            lambda *refs: round_kernel(places, acc is None, *refs),
            out_shape=jax.ShapeDtypeStruct((rows_dev, columns), f32),
            in_specs=specs,
            out_specs=in_vmem,
            scratch_shapes=[
                pltpu.VMEM((n * depth, rows_dev), bf16),
                pltpu.VMEM((n * depth, columns), bf16),
                pltpu.SemaphoreType.DMA((4 * n,)),
            ],
            input_output_aliases={} if acc is None else {n + 3: 0},
            compiler_params=params(20),
            cost_estimate=cost(2 * rows_dev * n * depth * columns, 4_000_000),
            name="round_of_%d" % n,
        )(*given)

    blocks = {(0, 0): tokens.T}
    acc = None
    held = [(0, 0)]
    for number, sends in enumerate(ROUNDS):
        fresh = {}
        for place, way in sends:
            fresh[moved(place, way)] = lax.ppermute({**blocks, **fresh}[place], "mp", pairs_of(way))
        if number > 0:
            acc = multiply(held, acc)
            held = []
        held += list(fresh)
        blocks.update(fresh)

    n = len(held)
    message = pl.pallas_call(
        lambda *refs: last_kernel(held, *refs),
        out_shape=jax.ShapeDtypeStruct((device_total, 128), f32),
        in_specs=[any_space] * (n + 3) + [in_vmem, any_space] + [in_vmem] * 3,
        out_specs=in_vmem,
        scratch_shapes=[
            pltpu.VMEM((n * depth, rows_dev), bf16),
            pltpu.VMEM((n * depth, columns), bf16),
            pltpu.VMEM((rows_dev, width), bf16),
            pltpu.VMEM((256, 2 * width), f32),
            pltpu.VMEM((256, 2 * width), f32),
            pltpu.VMEM((2, pairs_dev, width), f32),
            pltpu.SemaphoreType.DMA((4 * n,)),
            pltpu.SemaphoreType.DMA((rows_dev // 256,)),
        ],
        compiler_params=params(24),
        cost_estimate=cost(2 * rows_dev * n * depth * columns, 12_000_000),
        name="last_round",
    )(*[blocks[place] for place in held], gate_weight, up_weight, table, acc, target, unit_weight[None, :], gate_out, up_out)

    received = lax.all_to_all(message, ("pop", "mp"), 0, 0, tiled=True)

    left_rows = model_width // lax.axis_size("pop")
    left_gate, left_up, right_gate, right_up = pl.pallas_call(
        factor_kernel,
        out_shape=[jax.ShapeDtypeStruct((left_rows, pair_total * 4), bf16)] * 2
        + [jax.ShapeDtypeStruct((pair_total * 4, width), bf16)] * 2,
        in_specs=[in_vmem] * 2,
        out_specs=[in_vmem] * 4,
        compiler_params=params(8),
        cost_estimate=cost(3_000_000_000, 4_000_000),
        name="factor_tables",
    )(after(right_columns, message), left_lanes)
    update_gate, update_up, fitness = pl.pallas_call(
        update_kernel,
        out_shape=[jax.ShapeDtypeStruct((left_rows, width), f32)] * 2
        + [jax.ShapeDtypeStruct((1, 2 * pairs_dev), f32)],
        in_specs=[in_vmem] * 3 + [any_space] * 2,
        out_specs=[in_vmem] * 3,
        scratch_shapes=[
            pltpu.VMEM((16, 128), f32),
            pltpu.VMEM((pair_total * 4, width), bf16),
            pltpu.VMEM((pair_total * 4, width), bf16),
            pltpu.SemaphoreType.DMA((2,)),
        ],
        compiler_params=params(16),
        cost_estimate=cost(1_200_000_000, 5_000_000),
        name="update",
    )(received, left_gate, left_up, right_gate, right_up)
    return (update_gate, update_up, fitness.reshape(2 * pairs_dev))


def solution(mesh):
    return jax.shard_map(
        on_device,
        mesh=mesh,
        in_specs=(P("pop", "mp"), P("pop", "mp"), P("mp"), P(None, "mp"), P(None, "mp"), P()),
        out_specs=(P("pop", "mp"), P("pop", "mp"), P("pop")),
        check_vma=False,
    )
```

```python
import math

import jax
import jax.numpy as jnp
from jax import lax
from jax.experimental import pallas as pl
from jax.experimental.pallas import tpu as pltpu
from jax.sharding import PartitionSpec as P

FF = 10240
ROWS = 64
SIGMA = 0.5
EPSILON = 1e-05
SEED_STEP = 747796405
CELL_STEP = 277803737

WAYS = {"+x": (1, 0), "-x": (3, 0), "+y": (0, 1), "-y": (0, 3)}
ROUNDS = (
    (((0, 0), "+x"), ((0, 0), "-y"), ((0, 0), "-x"), ((0, 0), "+y")),
    (((1, 0), "+x"), ((0, 3), "-y"), ((0, 3), "-x"), ((1, 0), "+y")),
    (((0, 3), "+x"), ((2, 0), "-y"), ((0, 1), "-x"), ((2, 0), "+y")),
    (((0, 2), "+x"), ((0, 2), "-x"), ((2, 3), "-y")),
)


def moved(place, way):
    return ((place[0] + WAYS[way][0]) % 4, (place[1] + WAYS[way][1]) % 4)


def pairs_of(way):
    dx, dy = WAYS[way]
    return [(y * 4 + x, (y + dy) % 4 * 4 + (x + dx) % 4) for y in range(4) for x in range(4)]


def source_of(place):
    me = lax.axis_index("mp")
    return lax.rem(me // 4 + 4 - place[1], 4) * 4 + lax.rem(lax.rem(me, 4) + 4 - place[0], 4)


def levels_of(mixed):
    mixed = jnp.bitwise_xor(mixed, jnp.right_shift(mixed, 15))
    mixed = mixed * 1664525 + 1013904223
    mixed = jnp.bitwise_xor(mixed, jnp.right_shift(mixed, 13))
    level = jnp.bitwise_and(mixed, 255).astype(jnp.float32) * (2.0 / 256.0) - 255.0 / 256.0
    return level.astype(jnp.bfloat16)


def iota(shape, dim):
    return lax.broadcasted_iota(jnp.int32, shape, dim)


def by_pair(shape, dim, pairs, seed_ref, first_pair):
    at = iota(shape, dim)
    mixed = lax.rem(at, 4) * CELL_STEP
    for p in range(pairs):
        mixed += jnp.where(at // 4 == p, seed_ref[first_pair + p] * SEED_STEP, 0)
    return mixed


def prepare_kernel(seed_ref, table_ref, gate_ref, up_ref):
    width = gate_ref.shape[1]
    first_pair = lax.axis_index("pop") * 16
    lane = iota((1, 128), 1)
    half = lax.rem(lane, 4) * CELL_STEP + jnp.where(lane >= 64, 33023, 11003)
    for p in range(16):
        half += jnp.where(lax.rem(lane, 64) // 4 == p, seed_ref[first_pair + p] * SEED_STEP, 0)

    @pl.loop(0, table_ref.shape[0] // 32)
    def _(r):
        at = pl.multiple_of(r * 32, 32)
        cell = (iota((32, 128), 0) + at) * (4 * CELL_STEP)
        table_ref[pl.ds(at, 32), :] = levels_of(half + cell)

    first_unit = lax.axis_index("mp") * width
    cell = (iota((16, width), 1) + first_unit) * (4 * CELL_STEP)
    nothing = jnp.zeros((64, width), jnp.bfloat16)
    for i in range(4):
        column = by_pair((16, width), 0, 4, seed_ref, first_pair + 4 * i)
        gate = levels_of(column + cell + 22013)
        up = levels_of(column + cell + 44041)
        for part in (0, 128):
            gate_ref[part + i * 16 : part + i * 16 + 16, :] = gate
            up_ref[part + 64 + i * 16 : part + 64 + i * 16 + 16, :] = up
    for part in (0, 128):
        gate_ref[part + 64 : part + 128, :] = nothing
        up_ref[part : part + 64, :] = nothing


def factor_kernel(seed_ref, message_ref, table_ref, lane_ref):
    pairs = seed_ref.shape[0]
    width = table_ref.shape[1] // 2
    count = (table_ref.shape[0] - 4 * pairs) // 2
    first = lax.axis_index("mp") * width
    rows = 16
    cell = (iota((rows, width), 1) + first) * (4 * CELL_STEP)

    @pl.loop(0, 4 * pairs // rows)
    def _(i):
        at = pl.multiple_of(i * rows, rows)
        column = by_pair((rows, 128), 0, 4, seed_ref, i * 4)
        mixed = jnp.concatenate([column] * (width // 128), axis=1) + cell
        table_ref[pl.ds(at, rows), :width] = levels_of(mixed + 22013)
        table_ref[pl.ds(at, rows), width:] = levels_of(mixed + 44041)

    left_first = lax.axis_index("pop") * count

    @pl.loop(0, 4 * pairs // 128)
    def _(q):
        lane_ref[...] = jnp.broadcast_to(by_pair((1, 128), 1, 32, seed_ref, q * 32), lane_ref.shape)
        columns = pl.ds(pl.multiple_of(q * 128, 128), 128)

        @pl.loop(0, count // 32)
        def _(i):
            at = pl.multiple_of(i * 32, 32)
            mixed = (iota((32, 128), 0) + (at + left_first)) * (4 * CELL_STEP) + lane_ref[0:1, :]
            table_ref[pl.ds(4 * pairs + at, 32), columns] = levels_of(mixed + 11003)
            table_ref[pl.ds(4 * pairs + count + at, 32), columns] = levels_of(mixed + 33023)


def contract(a, b):
    return lax.dot_general(a, b, (((0,), (0,)), ((), ())), preferred_element_type=jnp.float32)


def product_of(places, blocks, rows, gate_ref, up_ref, table_ref):
    depth = blocks[0].shape[0]
    tokens = jnp.concatenate([block[:, rows] for block in blocks], axis=0)
    weights = []
    for place in places:
        at = pl.ds(pl.multiple_of(source_of(place) * depth, 32), depth)
        weights.append(jnp.concatenate([gate_ref[at, :], up_ref[at, :], table_ref[at, :]], axis=1))
    return contract(tokens, jnp.concatenate(weights, axis=0))


def round_kernel(places, fresh, *refs):
    n = len(places)
    acc_ref, mark_ref = refs[-2:]
    mark_ref[...] = jnp.zeros_like(mark_ref)

    @pl.loop(0, acc_ref.shape[0] // 256)
    def _(i):
        rows = pl.ds(pl.multiple_of(i * 256, 256), 256)
        part = product_of(places, refs[:n], rows, *refs[n : n + 3])
        if fresh:
            acc_ref[rows, :] = part
        else:
            acc_ref[rows, :] = refs[n + 3][rows, :] + part


def last_kernel(places, *refs):
    n = len(places)
    blocks, weight_refs = refs[:n], refs[n : n + 3]
    acc_ref, target_ref, weight_ref, gate_out_ref, up_out_ref, message_ref = refs[n + 3 : n + 9]
    total_refs, side_refs, parts_ref = refs[n + 9 : n + 11], refs[n + 11 : n + 13], refs[n + 13]
    depth = blocks[0].shape[0]
    width = target_ref.shape[1]
    tile = 256
    tiles = acc_ref.shape[0] // tile
    scale = SIGMA / math.sqrt(16 * depth)
    lane_pair = lax.rem(iota((tile, 128), 1), 64) // 4
    row_pair = iota((tile, 128), 0) // ROWS

    def product(i):
        rows = pl.ds(i * tile, tile)
        part = product_of(places, blocks, rows, *weight_refs) + acc_ref[rows, :]
        total_refs[i % 2][...] = part[:, : 2 * width]
        low = jnp.where(lane_pair == row_pair + i * (tile // ROWS), part[:, 2 * width :] * scale, 0.0)
        high = low.astype(jnp.bfloat16)
        rest = (low - high.astype(jnp.float32)).astype(jnp.bfloat16)
        low_both = jnp.concatenate([high, rest], axis=1)
        side_refs[i % 2][:, :width] = jnp.dot(low_both, gate_out_ref[...], preferred_element_type=jnp.float32)
        side_refs[i % 2][:, width:] = jnp.dot(low_both, up_out_ref[...], preferred_element_type=jnp.float32)

    def errors(i):
        total_ref, side_ref = total_refs[i % 2], side_refs[i % 2]
        for p in range(tile // ROWS):
            k = i * (tile // ROWS) + p
            plus = jnp.zeros((8, width), jnp.float32)
            minus = jnp.zeros((8, width), jnp.float32)
            for q in range(ROWS // 16):
                at = p * ROWS + q * 16
                goals = target_ref[i * tile + at : i * tile + at + 16, :].astype(jnp.float32)
                for h in range(2):
                    here = slice(at + h * 8, at + h * 8 + 8)
                    goal = goals[h * 8 : h * 8 + 8, :]
                    gate, up = total_ref[here, :width], total_ref[here, width:]
                    side_gate, side_up = side_ref[here, :width], side_ref[here, width:]
                    half = 0.5 * (gate + side_gate)
                    error = (half * jnp.tanh(half) + half) * (up + side_up) - goal
                    plus += error * error
                    half = 0.5 * (gate - side_gate)
                    error = (half * jnp.tanh(half) + half) * (up - side_up) - goal
                    minus += error * error
            parts_ref[0, k : k + 1, :] = jnp.sum(plus, axis=0, keepdims=True) * weight_ref[...][None, :]
            parts_ref[1, k : k + 1, :] = jnp.sum(minus, axis=0, keepdims=True) * weight_ref[...][None, :]

    product(0)
    for i in range(tiles):
        if i + 1 < tiles:
            product(i + 1)
        errors(i)

    pairs = parts_ref.shape[1]
    lane = iota((pairs, 128), 1)
    pair = iota((pairs, 128), 0)
    line = jnp.zeros((1, 128), jnp.float32)
    for s in range(2):
        sums = jnp.sum(parts_ref[s], axis=1, keepdims=True) * (1.0 / (ROWS * FF))
        line += jnp.sum(jnp.where(lane // 4 == pair + 16 * s, sums, 0.0), axis=0, keepdims=True)
    message_ref[...] = jnp.broadcast_to(line, message_ref.shape)


def update_kernel(message_ref, table_hbm, out_gate_ref, out_up_ref, fit_ref, f_ref, table_ref, sems):
    rows, width = out_gate_ref.shape
    depth = table_ref.shape[0] - 2 * rows
    parts = []
    for k in range(2):
        left, right = pl.ds(depth + k * rows, rows), (pl.ds(0, depth), pl.ds(k * width, width))
        parts.append(pltpu.make_async_copy(table_hbm.at[left, :], table_ref.at[left, :], sems.at[2 * k]))
        parts.append(pltpu.make_async_copy(table_hbm.at[right], table_ref.at[right], sems.at[2 * k + 1]))
    for copy in parts:
        copy.start()
    count = message_ref.shape[0]
    pick_row, pick = iota((16, count), 0), iota((16, count), 1)
    chosen = pick // 16 == 2 * lax.rem(pick_row, 8) + pick_row // 8
    by_pop = jnp.dot(
        chosen.astype(jnp.float32),
        message_ref[...],
        precision=lax.Precision.HIGHEST,
        preferred_element_type=jnp.float32,
    )
    even, odd = by_pop[:8], by_pop[8:]
    low_lane = iota((8, 128), 1) < 64
    plus = jnp.where(low_lane, even, pltpu.roll(odd, 64, 1))
    minus = jnp.where(low_lane, pltpu.roll(even, 64, 1), odd)
    summed = jnp.concatenate([plus, minus], axis=0)
    scores = -summed
    members = 4.0 * 512.0
    center = jnp.sum(scores) / members
    spread = jnp.sum((scores - center) ** 2) / members
    fitness = (scores - center) / jnp.sqrt(jnp.full((16, 128), spread + EPSILON, jnp.float32))
    f_ref[...] = fitness
    factor = (fitness[:8] - fitness[8:]) * (0.5 / 16.0)
    for k, out_ref in enumerate((out_gate_ref, out_up_ref)):
        parts[2 * k].wait()
        highs, rests = [], []
        for q in range(8):
            left = table_ref[depth + k * rows : depth + (k + 1) * rows, q * 128 : (q + 1) * 128]
            scaled = left.astype(jnp.float32) * factor[q : q + 1, :]
            high = scaled.astype(jnp.bfloat16)
            highs.append(high)
            rests.append((scaled - high.astype(jnp.float32)).astype(jnp.bfloat16))
        both = jnp.concatenate([jnp.concatenate(highs, axis=1), jnp.concatenate(rests, axis=1)], axis=0)
        parts[2 * k + 1].wait()
        right = table_ref[:depth, k * width : (k + 1) * width]
        product = jnp.dot(both, right, preferred_element_type=jnp.float32)
        out_ref[...] = product[:rows] + product[rows:]
    pop = lax.axis_index("pop")
    mine = pop // 2
    lane, member = iota((128, 128), 0), iota((128, 128), 1)
    at = lane == lax.rem(pop, 2) * 64 + member // 2 * 4
    total = jnp.zeros((1, 128), jnp.float32)
    for s in range(2):
        line = jnp.broadcast_to(f_ref[pl.ds(mine + 8 * s, 1), :], (8, 128))
        select = (at & (lax.rem(member, 2) == s)).astype(jnp.float32)
        total += jnp.dot(line, select, precision=lax.Precision.HIGHEST, preferred_element_type=jnp.float32)[:1]
    fit_ref[...] = total[:, : fit_ref.shape[1]]


def params(mib):
    return pltpu.CompilerParams(vmem_limit_bytes=mib * 1024 * 1024)


def cost(flops, size):
    return pl.CostEstimate(flops=flops, bytes_accessed=size, transcendentals=0)


def after(value, other):
    return lax.optimization_barrier((value, other))[0]


def on_device(tokens, target, unit_weight, gate_weight, up_weight, seeds):
    rows_dev, depth = tokens.shape
    model_width, width = gate_weight.shape
    pairs_dev = rows_dev // ROWS
    pair_total = seeds.shape[0]
    device_total = lax.axis_size("pop") * lax.axis_size("mp")
    any_space = pl.BlockSpec(memory_space=pl.ANY)
    in_vmem = pl.BlockSpec(memory_space=pltpu.VMEM)
    bf16, f32 = jnp.bfloat16, jnp.float32

    in_smem = pl.BlockSpec(memory_space=pltpu.SMEM)
    columns = 2 * width + 128

    table, gate_out, up_out = pl.pallas_call(
        prepare_kernel,
        out_shape=[jax.ShapeDtypeStruct((model_width, 128), bf16)] + [jax.ShapeDtypeStruct((256, width), bf16)] * 2,
        in_specs=[in_smem],
        out_specs=[in_vmem] * 3,
        compiler_params=params(6),
        cost_estimate=cost(2_000_000_000, 2_000_000),
        name="prepare",
    )(seeds)
    weights = [gate_weight, up_weight, table]

    def multiply(places, acc):
        given = [blocks[place] for place in places] + weights + ([] if acc is None else [acc])
        return pl.pallas_call(
            lambda *refs: round_kernel(places, acc is None, *refs),
            out_shape=[jax.ShapeDtypeStruct((rows_dev, columns), f32), jax.ShapeDtypeStruct((8, 128), f32)],
            in_specs=[in_vmem] * len(given),
            out_specs=[in_vmem] * 2,
            input_output_aliases={} if acc is None else {len(given) - 1: 0},
            compiler_params=params(12),
            cost_estimate=cost(2 * rows_dev * len(places) * depth * columns, 4_000_000),
            name="round_of_%d" % len(places),
        )(*given)

    blocks = {(0, 0): tokens.T}
    acc, mark = None, gate_out
    held = [(0, 0)]
    for number, sends in enumerate(ROUNDS):
        fresh = {}
        for place, way in sends:
            block = blocks[place]
            if number > 0:
                block = after(block, mark)
            fresh[moved(place, way)] = lax.ppermute(block, "mp", pairs_of(way))
        if number > 0:
            acc, mark = multiply(held, acc)
            held = []
        held += list(fresh)
        blocks.update(fresh)

    message = pl.pallas_call(
        lambda *refs: last_kernel(held, *refs),
        out_shape=jax.ShapeDtypeStruct((device_total, 128), f32),
        in_specs=[in_vmem] * (len(held) + 8),
        out_specs=in_vmem,
        scratch_shapes=[pltpu.VMEM((256, 2 * width), f32)] * 4 + [pltpu.VMEM((2, pairs_dev, width), f32)],
        compiler_params=params(16),
        cost_estimate=cost(2 * rows_dev * len(held) * depth * columns, 12_000_000),
        name="last_round",
    )(*[blocks[place] for place in held], *weights, acc, target, unit_weight, gate_out, up_out)

    received = lax.all_to_all(message, ("pop", "mp"), 0, 0, tiled=True)

    left_rows = model_width // lax.axis_size("pop")
    factors = pl.pallas_call(
        factor_kernel,
        out_shape=jax.ShapeDtypeStruct((4 * pair_total + 2 * left_rows, 2 * width), bf16),
        in_specs=[in_smem, any_space],
        out_specs=in_vmem,
        scratch_shapes=[pltpu.VMEM((8, 128), jnp.int32)],
        compiler_params=params(8),
        cost_estimate=cost(3_000_000_000, 4_000_000),
        name="factor_tables",
    )(seeds, message)
    update_gate, update_up, fitness = pl.pallas_call(
        update_kernel,
        out_shape=[jax.ShapeDtypeStruct((left_rows, width), f32)] * 2
        + [jax.ShapeDtypeStruct((1, 2 * pairs_dev), f32)],
        in_specs=[in_vmem, any_space],
        out_specs=[in_vmem] * 3,
        scratch_shapes=[
            pltpu.VMEM((16, 128), f32),
            pltpu.VMEM(factors.shape, bf16),
            pltpu.SemaphoreType.DMA((4,)),
        ],
        compiler_params=params(58),
        cost_estimate=cost(1_200_000_000, 5_000_000),
        name="update",
    )(received, factors)
    return (update_gate, update_up, fitness.reshape(2 * pairs_dev))


def solution(mesh):
    return jax.shard_map(
        on_device,
        mesh=mesh,
        in_specs=(P("pop", "mp"), P("pop", "mp"), P("mp"), P(None, "mp"), P(None, "mp"), P()),
        out_specs=(P("pop", "mp"), P("pop", "mp"), P("pop")),
        check_vma=False,
    )
```

```python
import math

import jax
import jax.numpy as jnp
from jax import lax
from jax.experimental import pallas as pl
from jax.experimental.pallas import tpu as pltpu
from jax.sharding import PartitionSpec as P

FF = 10240
ROWS = 64
SIGMA = 0.5
EPSILON = 1e-05
SEED_STEP = 747796405
CELL_STEP = 277803737

WAYS = {"+x": (1, 0), "-x": (3, 0), "+y": (0, 1), "-y": (0, 3)}
ROUNDS = (
    (((0, 0), "+x"), ((0, 0), "-y"), ((0, 0), "-x"), ((0, 0), "+y")),
    (((1, 0), "+x"), ((0, 3), "-y"), ((0, 3), "-x"), ((1, 0), "+y")),
    (((0, 3), "+x"), ((2, 0), "-y"), ((0, 1), "-x"), ((2, 0), "+y")),
    (((0, 2), "+x"), ((0, 2), "-x")),
)
HALVES = (((2, 3), "-y"), ((2, 1), "+y"))


def moved(place, way):
    return ((place[0] + WAYS[way][0]) % 4, (place[1] + WAYS[way][1]) % 4)


def pairs_of(way):
    dx, dy = WAYS[way]
    return [(y * 4 + x, (y + dy) % 4 * 4 + (x + dx) % 4) for y in range(4) for x in range(4)]


def source_of(place):
    me = lax.axis_index("mp")
    return lax.rem(me // 4 + 4 - place[1], 4) * 4 + lax.rem(lax.rem(me, 4) + 4 - place[0], 4)


def bytes_of(mixed):
    mixed = jnp.bitwise_xor(mixed, jnp.right_shift(mixed, 15))
    mixed = mixed * 1664525 + 1013904223
    mixed = jnp.bitwise_xor(mixed, jnp.right_shift(mixed, 13))
    return jnp.bitwise_and(mixed, 255)


def levels_of(mixed):
    level = bytes_of(mixed).astype(jnp.float32) * (2.0 / 256.0) - 255.0 / 256.0
    return level.astype(jnp.bfloat16)


def iota(shape, dim):
    return lax.broadcasted_iota(jnp.int32, shape, dim)


def by_pair(shape, dim, pairs, seed_ref, first_pair):
    at = iota(shape, dim)
    mixed = lax.rem(at, 4) * CELL_STEP
    for p in range(pairs):
        mixed += jnp.where(at // 4 == p, seed_ref[first_pair + p] * SEED_STEP, 0)
    return mixed


def prepare_kernel(seed_ref, table_ref, gate_ref, up_ref):
    width = gate_ref.shape[1]
    first_pair = lax.axis_index("pop") * 16
    lane = iota((1, 128), 1)
    half = lax.rem(lane, 4) * CELL_STEP + jnp.where(lane >= 64, 33023, 11003)
    for p in range(16):
        half += jnp.where(lax.rem(lane, 64) // 4 == p, seed_ref[first_pair + p] * SEED_STEP, 0)

    @pl.loop(0, table_ref.shape[0] // 32)
    def _(r):
        at = pl.multiple_of(r * 32, 32)
        cell = (iota((32, 128), 0) + at) * (4 * CELL_STEP)
        table_ref[pl.ds(at, 32), :] = levels_of(half + cell)

    first_unit = lax.axis_index("mp") * width
    cell = (iota((16, width), 1) + first_unit) * (4 * CELL_STEP)
    nothing = jnp.zeros((64, width), jnp.bfloat16)
    for i in range(4):
        column = by_pair((16, width), 0, 4, seed_ref, first_pair + 4 * i)
        gate = levels_of(column + cell + 22013)
        up = levels_of(column + cell + 44041)
        for part in (0, 128):
            gate_ref[part + i * 16 : part + i * 16 + 16, :] = gate
            up_ref[part + 64 + i * 16 : part + 64 + i * 16 + 16, :] = up
    for part in (0, 128):
        gate_ref[part + 64 : part + 128, :] = nothing
        up_ref[part : part + 64, :] = nothing


def factor_kernel(seed_ref, message_ref, left_ref, table_ref, lane_ref):
    pairs = seed_ref.shape[0]
    width = table_ref.shape[1] // 2
    count = left_ref.shape[0] // 2
    first = lax.axis_index("mp") * width
    rows = 16
    cell = (iota((rows, width), 1) + first) * (4 * CELL_STEP)

    @pl.loop(0, 4 * pairs // rows)
    def _(i):
        at = pl.multiple_of(i * rows, rows)
        column = by_pair((rows, 128), 0, 4, seed_ref, i * 4)
        mixed = jnp.concatenate([column] * (width // 128), axis=1) + cell
        table_ref[pl.ds(at, rows), :width] = levels_of(mixed + 22013)
        table_ref[pl.ds(at, rows), width:] = levels_of(mixed + 44041)

    left_first = lax.axis_index("pop") * count

    @pl.loop(0, 4 * pairs // 128)
    def _(q):
        lane_ref[...] = jnp.broadcast_to(by_pair((1, 128), 1, 32, seed_ref, q * 32), lane_ref.shape)
        columns = pl.ds(pl.multiple_of(q * 128, 128), 128)

        @pl.loop(0, count // 32)
        def _(i):
            at = pl.multiple_of(i * 32, 32)
            mixed = (iota((32, 128), 0) + (at + left_first)) * (4 * CELL_STEP) + lane_ref[0:1, :]
            left_ref[pl.ds(at, 32), columns] = (bytes_of(mixed + 11003) - 128).astype(jnp.int8)
            left_ref[pl.ds(pl.multiple_of(count + at, 32), 32), columns] = (bytes_of(mixed + 33023) - 128).astype(jnp.int8)


def contract(a, b):
    return lax.dot_general(a, b, (((0,), (0,)), ((), ())), preferred_element_type=jnp.float32)


def product_of(places, blocks, rows, gate_ref, up_ref, table_ref):
    depth = blocks[0].shape[0]
    tokens = jnp.concatenate([block[:, rows] for block in blocks], axis=0)
    weights = []
    for place in places:
        at = pl.ds(pl.multiple_of(source_of(place) * depth, 32), depth)
        weights.append(jnp.concatenate([gate_ref[at, :], up_ref[at, :], table_ref[at, :]], axis=1))
    return contract(tokens, jnp.concatenate(weights, axis=0))


def round_kernel(places, fresh, *refs):
    n = len(places)
    acc_ref, mark_ref = refs[-2:]
    mark_ref[...] = jnp.zeros_like(mark_ref)

    @pl.loop(0, acc_ref.shape[0] // 256)
    def _(i):
        rows = pl.ds(pl.multiple_of(i * 256, 256), 256)
        part = product_of(places, refs[:n], rows, *refs[n : n + 3])
        if fresh:
            acc_ref[rows, :] = part
        else:
            acc_ref[rows, :] = refs[n + 3][rows, :] + part


def last_kernel(pieces, *refs):
    n = len(pieces)
    blocks, weight_refs = refs[:n], refs[n : n + 3]
    acc_ref, target_ref, weight_ref, gate_out_ref, up_out_ref, message_ref = refs[n + 3 : n + 9]
    total_refs, side_refs, (parts_ref, turned_ref, low_ref) = refs[n + 9 : n + 11], refs[n + 11 : n + 13], refs[n + 13 :]
    depth = blocks[0].shape[0]
    width = target_ref.shape[1]
    tile = 256
    tiles = acc_ref.shape[0] // tile
    scale = SIGMA / math.sqrt(16 * depth)
    features = [
        pl.ds(pl.multiple_of(source_of(place) * depth + offset, 16), block.shape[0])
        for (place, offset), block in zip(pieces, blocks)
    ]
    lane_pair = lax.rem(iota((tile, 128), 1), 64) // 4
    row_pair = iota((tile, 128), 0) // ROWS

    def weight_columns(low, high):
        gate_ref, up_ref = weight_refs[:2]
        cut = []
        for at in features:
            sides = []
            if low < width:
                sides.append(gate_ref[at, low : min(high, width)])
            if high > width:
                sides.append(up_ref[at, max(low, width) - width : high - width])
            cut.append(sides[0] if len(sides) == 1 else jnp.concatenate(sides, axis=1))
        return jnp.concatenate(cut, axis=0)

    def products(i):
        rows = pl.ds(i * tile, tile)
        total_ref, side_ref = total_refs[i % 2], side_refs[i % 2]

        def turn():
            turned_ref[...] = jnp.concatenate([block[:, rows] for block in blocks], axis=0).T
            table = jnp.concatenate([weight_refs[2][at, :] for at in features], axis=0)
            low = jnp.dot(turned_ref[...], table, preferred_element_type=jnp.float32) + acc_ref[rows, 2 * width :]
            low = jnp.where(lane_pair == row_pair + i * (tile // ROWS), low * scale, 0.0)
            high = low.astype(jnp.bfloat16)
            low_ref[:, :128] = high
            low_ref[:, 128:] = (low - high.astype(jnp.float32)).astype(jnp.bfloat16)

        def side(out_ref, first):
            def step():
                side_ref[:, first : first + width] = jnp.dot(low_ref[...], out_ref[...], preferred_element_type=jnp.float32)

            return step

        def total(low, high):
            def step():
                part = jnp.dot(turned_ref[...], weight_columns(low, high), preferred_element_type=jnp.float32)
                total_ref[:, low:high] = part + acc_ref[rows, low:high]

            return step

        return [turn, side(gate_out_ref, 0), side(up_out_ref, width)] + [
            total(low, low + 256) for low in range(0, 2 * width, 256)
        ]

    def errors(i):
        total_ref, side_ref = total_refs[i % 2], side_refs[i % 2]

        def of_pair(p, kept):
            k = i * (tile // ROWS) + p

            def of_rows(q):
                plus, minus = kept.get(p) or (jnp.zeros((8, width), jnp.float32), jnp.zeros((8, width), jnp.float32))
                at = p * ROWS + q * 16
                goals = target_ref[i * tile + at : i * tile + at + 16, :].astype(jnp.float32)
                for h in range(2):
                    here = slice(at + h * 8, at + h * 8 + 8)
                    goal = goals[h * 8 : h * 8 + 8, :]
                    gate, up = total_ref[here, :width], total_ref[here, width:]
                    side_gate, side_up = side_ref[here, :width], side_ref[here, width:]
                    half = 0.5 * (gate + side_gate)
                    error = (half * jnp.tanh(half) + half) * (up + side_up) - goal
                    plus += error * error
                    half = 0.5 * (gate - side_gate)
                    error = (half * jnp.tanh(half) + half) * (up - side_up) - goal
                    minus += error * error
                kept[p] = (plus, minus)
                if q == ROWS // 16 - 1:
                    parts_ref[0, k : k + 1, :] = jnp.sum(plus, axis=0, keepdims=True) * weight_ref[...][None, :]
                    parts_ref[1, k : k + 1, :] = jnp.sum(minus, axis=0, keepdims=True) * weight_ref[...][None, :]

            return [lambda q=q: of_rows(q) for q in range(ROWS // 16)]

        kept = {}
        return [step for p in range(tile // ROWS) for step in of_pair(p, kept)]

    for step in products(0):
        step()
    for i in range(tiles):
        ahead = products(i + 1) if i + 1 < tiles else []
        behind = errors(i)
        for at, step in enumerate(behind):
            for other in ahead[at * len(ahead) // len(behind) : (at + 1) * len(ahead) // len(behind)]:
                other()
            step()

    pairs = parts_ref.shape[1]
    lane = iota((pairs, 128), 1)
    pair = iota((pairs, 128), 0)
    line = jnp.zeros((1, 128), jnp.float32)
    for s in range(2):
        sums = jnp.sum(parts_ref[s], axis=1, keepdims=True) * (1.0 / (ROWS * FF))
        line += jnp.sum(jnp.where(lane // 4 == pair + 16 * s, sums, 0.0), axis=0, keepdims=True)
    message_ref[...] = jnp.broadcast_to(line, message_ref.shape)


def update_kernel(message_ref, left_ref, table_ref, out_gate, out_up, fit_ref, f_ref, out_gate_ref, out_up_ref, sems):
    rows, width = out_gate_ref.shape
    count = message_ref.shape[0]
    pick_row, pick = iota((16, count), 0), iota((16, count), 1)
    chosen = pick // 16 == 2 * lax.rem(pick_row, 8) + pick_row // 8
    by_pop = jnp.dot(
        chosen.astype(jnp.float32),
        message_ref[...],
        precision=lax.Precision.HIGHEST,
        preferred_element_type=jnp.float32,
    )
    even, odd = by_pop[:8], by_pop[8:]
    low_lane = iota((8, 128), 1) < 64
    plus = jnp.where(low_lane, even, pltpu.roll(odd, 64, 1))
    minus = jnp.where(low_lane, pltpu.roll(even, 64, 1), odd)
    summed = jnp.concatenate([plus, minus], axis=0)
    scores = -summed
    members = 4.0 * 512.0
    center = jnp.sum(scores) / members
    spread = jnp.sum((scores - center) ** 2) / members
    fitness = (scores - center) / jnp.sqrt(jnp.full((16, 128), spread + EPSILON, jnp.float32))
    f_ref[...] = fitness
    factor = (fitness[:8] - fitness[8:]) * (0.5 / 16.0)
    copies = []
    for k, (out_ref, out) in enumerate(((out_gate_ref, out_gate), (out_up_ref, out_up))):
        highs, rests = [], []
        for q in range(8):
            left = left_ref[k * rows : (k + 1) * rows, q * 128 : (q + 1) * 128]
            level = left.astype(jnp.int32).astype(jnp.float32) * (2.0 / 256.0) + 1.0 / 256.0
            scaled = level * factor[q : q + 1, :]
            high = scaled.astype(jnp.bfloat16)
            highs.append(high)
            rests.append((scaled - high.astype(jnp.float32)).astype(jnp.bfloat16))
        right = table_ref[:, k * width : (k + 1) * width]
        out_ref[...] = jnp.dot(
            jnp.concatenate(highs, axis=1), right, preferred_element_type=jnp.float32
        ) + jnp.dot(jnp.concatenate(rests, axis=1), right, preferred_element_type=jnp.float32)
        copies.append(pltpu.make_async_copy(out_ref, out, sems.at[k]))
        copies[-1].start()
    pop = lax.axis_index("pop")
    mine = pop // 2
    lane, member = iota((128, 128), 0), iota((128, 128), 1)
    at = lane == lax.rem(pop, 2) * 64 + member // 2 * 4
    total = jnp.zeros((1, 128), jnp.float32)
    for s in range(2):
        line = jnp.broadcast_to(f_ref[pl.ds(mine + 8 * s, 1), :], (8, 128))
        select = (at & (lax.rem(member, 2) == s)).astype(jnp.float32)
        total += jnp.dot(line, select, precision=lax.Precision.HIGHEST, preferred_element_type=jnp.float32)[:1]
    fit_ref[...] = total[:, : fit_ref.shape[1]]
    for copy in copies:
        copy.wait()


def params(mib):
    return pltpu.CompilerParams(vmem_limit_bytes=mib * 1024 * 1024)


def cost(flops, size):
    return pl.CostEstimate(flops=flops, bytes_accessed=size, transcendentals=0)


def after(value, other):
    return lax.optimization_barrier((value, other))[0]


def on_device(tokens, target, unit_weight, gate_weight, up_weight, seeds):
    rows_dev, depth = tokens.shape
    model_width, width = gate_weight.shape
    pairs_dev = rows_dev // ROWS
    pair_total = seeds.shape[0]
    device_total = lax.axis_size("pop") * lax.axis_size("mp")
    any_space = pl.BlockSpec(memory_space=pl.ANY)
    in_vmem = pl.BlockSpec(memory_space=pltpu.VMEM)
    bf16, f32 = jnp.bfloat16, jnp.float32

    in_smem = pl.BlockSpec(memory_space=pltpu.SMEM)
    columns = 2 * width + 128

    table, gate_out, up_out = pl.pallas_call(
        prepare_kernel,
        out_shape=[jax.ShapeDtypeStruct((model_width, 128), bf16)] + [jax.ShapeDtypeStruct((256, width), bf16)] * 2,
        in_specs=[in_smem],
        out_specs=[in_vmem] * 3,
        compiler_params=params(6),
        cost_estimate=cost(2_000_000_000, 2_000_000),
        name="prepare",
    )(seeds)
    weights = [gate_weight, up_weight, table]

    def multiply(places, acc):
        given = [blocks[place] for place in places] + weights + ([] if acc is None else [acc])
        return pl.pallas_call(
            lambda *refs: round_kernel(places, acc is None, *refs),
            out_shape=[jax.ShapeDtypeStruct((rows_dev, columns), f32), jax.ShapeDtypeStruct((8, 128), f32)],
            in_specs=[in_vmem] * len(given),
            out_specs=[in_vmem] * 2,
            input_output_aliases={} if acc is None else {len(given) - 1: 0},
            compiler_params=params(12),
            cost_estimate=cost(2 * rows_dev * len(places) * depth * columns, 4_000_000),
            name="round_of_%d" % len(places),
        )(*given)

    blocks = {(0, 0): tokens.T}
    acc, mark = None, gate_out
    held = [(0, 0)]
    for number, sends in enumerate(ROUNDS):
        fresh = {}
        for place, way in sends:
            block = blocks[place]
            if number > 0:
                block = after(block, mark)
            fresh[moved(place, way)] = lax.ppermute(block, "mp", pairs_of(way))
        if number > 0:
            acc, mark = multiply(held, acc)
            held = []
        held += list(fresh)
        blocks.update(fresh)

    half = depth // 2
    last = [blocks[place] for place in held]
    pieces = [(place, 0) for place in held]
    for k, (place, way) in enumerate(HALVES):
        last.append(lax.ppermute(blocks[place][k * half : (k + 1) * half], "mp", pairs_of(way)))
        pieces.append((moved(place, way), k * half))
    message = pl.pallas_call(
        lambda *refs: last_kernel(pieces, *refs),
        out_shape=jax.ShapeDtypeStruct((device_total, 128), f32),
        in_specs=[in_vmem] * (len(last) + 8),
        out_specs=in_vmem,
        scratch_shapes=[pltpu.VMEM((256, 2 * width), f32)] * 4
        + [
            pltpu.VMEM((2, pairs_dev, width), f32),
            pltpu.VMEM((256, sum(block.shape[0] for block in last)), bf16),
            pltpu.VMEM((256, 256), bf16),
        ],
        compiler_params=params(16),
        cost_estimate=cost(2 * rows_dev * 3 * depth * columns, 12_000_000),
        name="last_round",
    )(*last, *weights, acc, target, unit_weight, gate_out, up_out)

    received = lax.all_to_all(message, ("pop", "mp"), 0, 0, tiled=True)

    left_rows = model_width // lax.axis_size("pop")
    left, right = pl.pallas_call(
        factor_kernel,
        out_shape=[
            jax.ShapeDtypeStruct((2 * left_rows, 4 * pair_total), jnp.int8),
            jax.ShapeDtypeStruct((4 * pair_total, 2 * width), bf16),
        ],
        in_specs=[in_smem, any_space],
        out_specs=[in_vmem] * 2,
        scratch_shapes=[pltpu.VMEM((8, 128), jnp.int32)],
        compiler_params=params(8),
        cost_estimate=cost(3_000_000_000, 4_000_000),
        name="factor_tables",
    )(seeds, message)
    update = jax.ShapeDtypeStruct((left_rows, width), f32)
    update_gate, update_up, fitness = pl.pallas_call(
        update_kernel,
        out_shape=[update, update, jax.ShapeDtypeStruct((1, 2 * pairs_dev), f32)],
        in_specs=[in_vmem] * 3,
        out_specs=[any_space, any_space, in_vmem],
        scratch_shapes=[
            pltpu.VMEM((16, 128), f32),
            pltpu.VMEM(update.shape, f32),
            pltpu.VMEM(update.shape, f32),
            pltpu.SemaphoreType.DMA((2,)),
        ],
        compiler_params=params(16),
        cost_estimate=cost(1_200_000_000, 5_000_000),
        name="update",
    )(received, left, right)
    return (update_gate, update_up, fitness.reshape(2 * pairs_dev))


def solution(mesh):
    return jax.shard_map(
        on_device,
        mesh=mesh,
        in_specs=(P("pop", "mp"), P("pop", "mp"), P("mp"), P(None, "mp"), P(None, "mp"), P()),
        out_specs=(P("pop", "mp"), P("pop", "mp"), P("pop")),
        check_vma=False,
    )
```

```python
import math

import jax
import jax.numpy as jnp
from jax import lax
from jax.experimental import pallas as pl
from jax.experimental.pallas import tpu as pltpu
from jax.sharding import PartitionSpec as P

FF = 10240
ROWS = 64
SIGMA = 0.5
EPSILON = 1e-05
SEED_STEP = 747796405
CELL_STEP = 277803737

WAYS = {"+x": (1, 0), "-x": (3, 0), "+y": (0, 1), "-y": (0, 3)}
ROUNDS = (
    (((0, 0), "+x"), ((0, 0), "-y"), ((0, 0), "-x"), ((0, 0), "+y")),
    (((1, 0), "+x"), ((0, 3), "-y"), ((0, 3), "-x"), ((1, 0), "+y")),
    (((0, 3), "+x"), ((2, 0), "-y"), ((0, 1), "-x"), ((2, 0), "+y")),
    (((0, 2), "+x"), ((0, 2), "-x"), ((2, 3), "-y")),
)


def moved(place, way):
    return ((place[0] + WAYS[way][0]) % 4, (place[1] + WAYS[way][1]) % 4)


def pairs_of(way):
    dx, dy = WAYS[way]
    return [(y * 4 + x, (y + dy) % 4 * 4 + (x + dx) % 4) for y in range(4) for x in range(4)]


def source_of(place):
    me = lax.axis_index("mp")
    return lax.rem(me // 4 + 4 - place[1], 4) * 4 + lax.rem(lax.rem(me, 4) + 4 - place[0], 4)


def bytes_of(mixed):
    mixed = jnp.bitwise_xor(mixed, jnp.right_shift(mixed, 15))
    mixed = mixed * 1664525 + 1013904223
    mixed = jnp.bitwise_xor(mixed, jnp.right_shift(mixed, 13))
    return jnp.bitwise_and(mixed, 255)


def levels_of(mixed):
    level = bytes_of(mixed).astype(jnp.float32) * (2.0 / 256.0) - 255.0 / 256.0
    return level.astype(jnp.bfloat16)


def iota(shape, dim):
    return lax.broadcasted_iota(jnp.int32, shape, dim)


def by_pair(shape, dim, pairs, seed_ref, first_pair):
    at = iota(shape, dim)
    mixed = lax.rem(at, 4) * CELL_STEP
    for p in range(pairs):
        mixed += jnp.where(at // 4 == p, seed_ref[first_pair + p] * SEED_STEP, 0)
    return mixed


def prepare_kernel(seed_ref, table_ref, gate_ref, up_ref):
    width = gate_ref.shape[1]
    first_pair = lax.axis_index("pop") * 16
    lane = iota((1, 128), 1)
    half = lax.rem(lane, 4) * CELL_STEP + jnp.where(lane >= 64, 33023, 11003)
    for p in range(16):
        half += jnp.where(lax.rem(lane, 64) // 4 == p, seed_ref[first_pair + p] * SEED_STEP, 0)

    @pl.loop(0, table_ref.shape[0] // 32)
    def _(r):
        at = pl.multiple_of(r * 32, 32)
        cell = (iota((32, 128), 0) + at) * (4 * CELL_STEP)
        table_ref[pl.ds(at, 32), :] = levels_of(half + cell)

    first_unit = lax.axis_index("mp") * width
    cell = (iota((16, width), 1) + first_unit) * (4 * CELL_STEP)
    nothing = jnp.zeros((64, width), jnp.bfloat16)
    for i in range(4):
        column = by_pair((16, width), 0, 4, seed_ref, first_pair + 4 * i)
        gate = levels_of(column + cell + 22013)
        up = levels_of(column + cell + 44041)
        for part in (0, 128):
            gate_ref[part + i * 16 : part + i * 16 + 16, :] = gate
            up_ref[part + 64 + i * 16 : part + 64 + i * 16 + 16, :] = up
    for part in (0, 128):
        gate_ref[part + 64 : part + 128, :] = nothing
        up_ref[part : part + 64, :] = nothing


def factor_kernel(seed_ref, message_ref, left_ref, table_ref, lane_ref):
    pairs = seed_ref.shape[0]
    width = table_ref.shape[1] // 2
    count = left_ref.shape[0] // 2
    first = lax.axis_index("mp") * width
    rows = 16
    cell = (iota((rows, width), 1) + first) * (4 * CELL_STEP)

    @pl.loop(0, 4 * pairs // rows)
    def _(i):
        at = pl.multiple_of(i * rows, rows)
        column = by_pair((rows, 128), 0, 4, seed_ref, i * 4)
        mixed = jnp.concatenate([column] * (width // 128), axis=1) + cell
        table_ref[pl.ds(at, rows), :width] = levels_of(mixed + 22013)
        table_ref[pl.ds(at, rows), width:] = levels_of(mixed + 44041)

    left_first = lax.axis_index("pop") * count

    @pl.loop(0, 4 * pairs // 128)
    def _(q):
        lane_ref[...] = jnp.broadcast_to(by_pair((1, 128), 1, 32, seed_ref, q * 32), lane_ref.shape)
        columns = pl.ds(pl.multiple_of(q * 128, 128), 128)

        @pl.loop(0, count // 32)
        def _(i):
            at = pl.multiple_of(i * 32, 32)
            mixed = (iota((32, 128), 0) + (at + left_first)) * (4 * CELL_STEP) + lane_ref[0:1, :]
            left_ref[pl.ds(at, 32), columns] = (bytes_of(mixed + 11003) - 128).astype(jnp.int8)
            left_ref[pl.ds(pl.multiple_of(count + at, 32), 32), columns] = (bytes_of(mixed + 33023) - 128).astype(jnp.int8)


def contract(a, b):
    return lax.dot_general(a, b, (((0,), (0,)), ((), ())), preferred_element_type=jnp.float32)


def product_of(places, blocks, rows, gate_ref, up_ref, table_ref):
    depth = blocks[0].shape[0]
    tokens = jnp.concatenate([block[:, rows] for block in blocks], axis=0)
    weights = []
    for place in places:
        at = pl.ds(pl.multiple_of(source_of(place) * depth, 32), depth)
        weights.append(jnp.concatenate([gate_ref[at, :], up_ref[at, :], table_ref[at, :]], axis=1))
    return contract(tokens, jnp.concatenate(weights, axis=0))


def round_kernel(places, fresh, *refs):
    n = len(places)
    acc_ref, mark_ref = refs[-2:]
    mark_ref[...] = jnp.zeros_like(mark_ref)
    tile = 512

    @pl.loop(0, acc_ref.shape[0] // tile)
    def _(i):
        rows = pl.ds(pl.multiple_of(i * tile, tile), tile)
        part = product_of(places, refs[:n], rows, *refs[n : n + 3])
        if fresh:
            acc_ref[rows, :] = part
        else:
            acc_ref[rows, :] = refs[n + 3][rows, :] + part


def last_kernel(pieces, *refs):
    n = len(pieces)
    blocks, weight_refs = refs[:n], refs[n : n + 3]
    acc_ref, target_ref, weight_ref, gate_out_ref, up_out_ref, message_ref = refs[n + 3 : n + 9]
    total_refs, side_refs, (parts_ref, turned_ref, low_ref) = refs[n + 9 : n + 11], refs[n + 11 : n + 13], refs[n + 13 :]
    depth = blocks[0].shape[0]
    width = target_ref.shape[1]
    tile = 256
    tiles = acc_ref.shape[0] // tile
    scale = SIGMA / math.sqrt(16 * depth)
    features = [
        pl.ds(pl.multiple_of(source_of(place) * depth + offset, 16), block.shape[0])
        for (place, offset), block in zip(pieces, blocks)
    ]
    lane_pair = lax.rem(iota((tile, 128), 1), 64) // 4
    row_pair = iota((tile, 128), 0) // ROWS

    def weight_columns(low, high):
        gate_ref, up_ref = weight_refs[:2]
        cut = []
        for at in features:
            sides = []
            if low < width:
                sides.append(gate_ref[at, low : min(high, width)])
            if high > width:
                sides.append(up_ref[at, max(low, width) - width : high - width])
            cut.append(sides[0] if len(sides) == 1 else jnp.concatenate(sides, axis=1))
        return jnp.concatenate(cut, axis=0)

    def products(i):
        rows = pl.ds(i * tile, tile)
        total_ref, side_ref = total_refs[i % 2], side_refs[i % 2]

        def turn():
            turned_ref[...] = jnp.concatenate([block[:, rows] for block in blocks], axis=0).T
            table = jnp.concatenate([weight_refs[2][at, :] for at in features], axis=0)
            low = jnp.dot(turned_ref[...], table, preferred_element_type=jnp.float32) + acc_ref[rows, 2 * width :]
            low = jnp.where(lane_pair == row_pair + i * (tile // ROWS), low * scale, 0.0)
            high = low.astype(jnp.bfloat16)
            low_ref[:, :128] = high
            low_ref[:, 128:] = (low - high.astype(jnp.float32)).astype(jnp.bfloat16)

        def side(out_ref, first):
            def step():
                side_ref[:, first : first + width] = jnp.dot(low_ref[...], out_ref[...], preferred_element_type=jnp.float32)

            return step

        def total(low, high):
            def step():
                part = jnp.dot(turned_ref[...], weight_columns(low, high), preferred_element_type=jnp.float32)
                total_ref[:, low:high] = part + acc_ref[rows, low:high]

            return step

        return [turn, side(gate_out_ref, 0), side(up_out_ref, width)] + [
            total(low, low + 256) for low in range(0, 2 * width, 256)
        ]

    def errors(i):
        total_ref, side_ref = total_refs[i % 2], side_refs[i % 2]

        def of_pair(p, kept):
            k = i * (tile // ROWS) + p

            def of_rows(q):
                plus, minus = kept.get(p) or (jnp.zeros((8, width), jnp.float32), jnp.zeros((8, width), jnp.float32))
                at = p * ROWS + q * 16
                goals = target_ref[i * tile + at : i * tile + at + 16, :].astype(jnp.float32)
                for h in range(2):
                    here = slice(at + h * 8, at + h * 8 + 8)
                    goal = goals[h * 8 : h * 8 + 8, :]
                    gate, up = total_ref[here, :width], total_ref[here, width:]
                    side_gate, side_up = side_ref[here, :width], side_ref[here, width:]
                    half = 0.5 * (gate + side_gate)
                    error = (half * jnp.tanh(half) + half) * (up + side_up) - goal
                    plus += error * error
                    half = 0.5 * (gate - side_gate)
                    error = (half * jnp.tanh(half) + half) * (up - side_up) - goal
                    minus += error * error
                kept[p] = (plus, minus)
                if q == ROWS // 16 - 1:
                    parts_ref[0, k : k + 1, :] = jnp.sum(plus, axis=0, keepdims=True) * weight_ref[...][None, :]
                    parts_ref[1, k : k + 1, :] = jnp.sum(minus, axis=0, keepdims=True) * weight_ref[...][None, :]

            return [lambda q=q: of_rows(q) for q in range(ROWS // 16)]

        kept = {}
        return [step for p in range(tile // ROWS) for step in of_pair(p, kept)]

    for step in products(0):
        step()
    for i in range(tiles):
        ahead = products(i + 1) if i + 1 < tiles else []
        behind = errors(i)
        for at, step in enumerate(behind):
            for other in ahead[at * len(ahead) // len(behind) : (at + 1) * len(ahead) // len(behind)]:
                other()
            step()

    pairs = parts_ref.shape[1]
    lane = iota((pairs, 128), 1)
    pair = iota((pairs, 128), 0)
    line = jnp.zeros((1, 128), jnp.float32)
    for s in range(2):
        sums = jnp.sum(parts_ref[s], axis=1, keepdims=True) * (1.0 / (ROWS * FF))
        line += jnp.sum(jnp.where(lane // 4 == pair + 16 * s, sums, 0.0), axis=0, keepdims=True)
    message_ref[...] = jnp.broadcast_to(line, message_ref.shape)


def update_kernel(message_ref, left_ref, table_ref, out_gate, out_up, fit_ref, f_ref, out_gate_ref, out_up_ref, sems):
    rows, width = out_gate_ref.shape
    count = message_ref.shape[0]
    pick_row, pick = iota((16, count), 0), iota((16, count), 1)
    chosen = pick // 16 == 2 * lax.rem(pick_row, 8) + pick_row // 8
    by_pop = jnp.dot(
        chosen.astype(jnp.float32),
        message_ref[...],
        precision=lax.Precision.HIGHEST,
        preferred_element_type=jnp.float32,
    )
    even, odd = by_pop[:8], by_pop[8:]
    low_lane = iota((8, 128), 1) < 64
    plus = jnp.where(low_lane, even, pltpu.roll(odd, 64, 1))
    minus = jnp.where(low_lane, pltpu.roll(even, 64, 1), odd)
    summed = jnp.concatenate([plus, minus], axis=0)
    scores = -summed
    members = 4.0 * 512.0
    center = jnp.sum(scores) / members
    spread = jnp.sum((scores - center) ** 2) / members
    fitness = (scores - center) / jnp.sqrt(jnp.full((16, 128), spread + EPSILON, jnp.float32))
    f_ref[...] = fitness
    factor = (fitness[:8] - fitness[8:]) * (0.5 / 16.0)
    copies = []
    for k, (out_ref, out) in enumerate(((out_gate_ref, out_gate), (out_up_ref, out_up))):
        highs, rests = [], []
        for q in range(8):
            left = left_ref[k * rows : (k + 1) * rows, q * 128 : (q + 1) * 128]
            level = left.astype(jnp.int32).astype(jnp.float32) * (2.0 / 256.0) + 1.0 / 256.0
            scaled = level * factor[q : q + 1, :]
            high = scaled.astype(jnp.bfloat16)
            highs.append(high)
            rests.append((scaled - high.astype(jnp.float32)).astype(jnp.bfloat16))
        right = table_ref[:, k * width : (k + 1) * width]
        out_ref[...] = jnp.dot(
            jnp.concatenate(highs, axis=1), right, preferred_element_type=jnp.float32
        ) + jnp.dot(jnp.concatenate(rests, axis=1), right, preferred_element_type=jnp.float32)
        copies.append(pltpu.make_async_copy(out_ref, out, sems.at[k]))
        copies[-1].start()
    pop = lax.axis_index("pop")
    mine = pop // 2
    lane, member = iota((128, 128), 0), iota((128, 128), 1)
    at = lane == lax.rem(pop, 2) * 64 + member // 2 * 4
    total = jnp.zeros((1, 128), jnp.float32)
    for s in range(2):
        line = jnp.broadcast_to(f_ref[pl.ds(mine + 8 * s, 1), :], (8, 128))
        select = (at & (lax.rem(member, 2) == s)).astype(jnp.float32)
        total += jnp.dot(line, select, precision=lax.Precision.HIGHEST, preferred_element_type=jnp.float32)[:1]
    fit_ref[...] = total[:, : fit_ref.shape[1]]
    for copy in copies:
        copy.wait()


def params(mib):
    return pltpu.CompilerParams(vmem_limit_bytes=mib * 1024 * 1024)


def cost(flops, size):
    return pl.CostEstimate(flops=flops, bytes_accessed=size, transcendentals=0)


def after(value, other):
    return lax.optimization_barrier((value, other))[0]


def on_device(tokens, target, unit_weight, gate_weight, up_weight, seeds):
    rows_dev, depth = tokens.shape
    model_width, width = gate_weight.shape
    pairs_dev = rows_dev // ROWS
    pair_total = seeds.shape[0]
    device_total = lax.axis_size("pop") * lax.axis_size("mp")
    any_space = pl.BlockSpec(memory_space=pl.ANY)
    in_vmem = pl.BlockSpec(memory_space=pltpu.VMEM)
    bf16, f32 = jnp.bfloat16, jnp.float32

    in_smem = pl.BlockSpec(memory_space=pltpu.SMEM)
    columns = 2 * width + 128

    table, gate_out, up_out = pl.pallas_call(
        prepare_kernel,
        out_shape=[jax.ShapeDtypeStruct((model_width, 128), bf16)] + [jax.ShapeDtypeStruct((256, width), bf16)] * 2,
        in_specs=[in_smem],
        out_specs=[in_vmem] * 3,
        compiler_params=params(6),
        cost_estimate=cost(2_000_000_000, 2_000_000),
        name="prepare",
    )(seeds)
    weights = [gate_weight, up_weight, table]

    def multiply(places, acc):
        given = [blocks[place] for place in places] + weights + ([] if acc is None else [acc])
        return pl.pallas_call(
            lambda *refs: round_kernel(places, acc is None, *refs),
            out_shape=[jax.ShapeDtypeStruct((rows_dev, columns), f32), jax.ShapeDtypeStruct((8, 128), f32)],
            in_specs=[in_vmem] * len(given),
            out_specs=[in_vmem] * 2,
            input_output_aliases={} if acc is None else {len(given) - 1: 0},
            compiler_params=params(12),
            cost_estimate=cost(2 * rows_dev * len(places) * depth * columns, 4_000_000),
            name="round_of_%d" % len(places),
        )(*given)

    blocks = {(0, 0): tokens.T}
    acc, mark = None, gate_out
    held = [(0, 0)]
    for number, sends in enumerate(ROUNDS):
        fresh = {}
        for place, way in sends:
            block = blocks[place]
            if number > 0:
                block = after(block, mark)
            fresh[moved(place, way)] = lax.ppermute(block, "mp", pairs_of(way))
        if number > 0:
            acc, mark = multiply(held, acc)
            held = []
        held += list(fresh)
        blocks.update(fresh)

    last = [blocks[place] for place in held]
    pieces = [(place, 0) for place in held]
    message = pl.pallas_call(
        lambda *refs: last_kernel(pieces, *refs),
        out_shape=jax.ShapeDtypeStruct((device_total, 128), f32),
        in_specs=[in_vmem] * (len(last) + 8),
        out_specs=in_vmem,
        scratch_shapes=[pltpu.VMEM((256, 2 * width), f32)] * 4
        + [
            pltpu.VMEM((2, pairs_dev, width), f32),
            pltpu.VMEM((256, sum(block.shape[0] for block in last)), bf16),
            pltpu.VMEM((256, 256), bf16),
        ],
        compiler_params=params(16),
        cost_estimate=cost(2 * rows_dev * 3 * depth * columns, 12_000_000),
        name="last_round",
    )(*last, *weights, acc, target, unit_weight, gate_out, up_out)

    received = lax.all_to_all(message, ("pop", "mp"), 0, 0, tiled=True)

    left_rows = model_width // lax.axis_size("pop")
    left, right = pl.pallas_call(
        factor_kernel,
        out_shape=[
            jax.ShapeDtypeStruct((2 * left_rows, 4 * pair_total), jnp.int8),
            jax.ShapeDtypeStruct((4 * pair_total, 2 * width), bf16),
        ],
        in_specs=[in_smem, any_space],
        out_specs=[in_vmem] * 2,
        scratch_shapes=[pltpu.VMEM((8, 128), jnp.int32)],
        compiler_params=params(8),
        cost_estimate=cost(3_000_000_000, 4_000_000),
        name="factor_tables",
    )(seeds, message)
    update = jax.ShapeDtypeStruct((left_rows, width), f32)
    update_gate, update_up, fitness = pl.pallas_call(
        update_kernel,
        out_shape=[update, update, jax.ShapeDtypeStruct((1, 2 * pairs_dev), f32)],
        in_specs=[in_vmem] * 3,
        out_specs=[any_space, any_space, in_vmem],
        scratch_shapes=[
            pltpu.VMEM((16, 128), f32),
            pltpu.VMEM(update.shape, f32),
            pltpu.VMEM(update.shape, f32),
            pltpu.SemaphoreType.DMA((2,)),
        ],
        compiler_params=params(16),
        cost_estimate=cost(1_200_000_000, 5_000_000),
        name="update",
    )(received, left, right)
    return (update_gate, update_up, fitness.reshape(2 * pairs_dev))


def solution(mesh):
    return jax.shard_map(
        on_device,
        mesh=mesh,
        in_specs=(P("pop", "mp"), P("pop", "mp"), P("mp"), P(None, "mp"), P(None, "mp"), P()),
        out_specs=(P("pop", "mp"), P("pop", "mp"), P("pop")),
        check_vma=False,
    )
```

```python
import math

import jax
import jax.numpy as jnp
from jax import lax
from jax.experimental import pallas as pl
from jax.experimental.pallas import tpu as pltpu
from jax.sharding import PartitionSpec as P

FF = 10240
ROWS = 64
SIGMA = 0.5
EPSILON = 1e-05
SEED_STEP = 747796405
CELL_STEP = 277803737

PASSED = (((0, 1),), ((0, 2), (3, 3), (1, 1)), ())
WAYS = {"+x": (1, 0), "-x": (3, 0), "+y": (0, 1), "-y": (0, 3)}
ROUNDS = (
    (((0, 0), "+x"), ((0, 0), "-y"), ((0, 0), "-x"), ((0, 0), "+y")),
    (((1, 0), "+x"), ((0, 3), "-y"), ((0, 3), "-x"), ((1, 0), "+y")),
    (((0, 3), "+x"), ((2, 0), "-y"), ((0, 1), "-x"), ((2, 0), "+y")),
    (((0, 2), "+x"), ((0, 2), "-x")),
)
HALVES = (((2, 3), (3, 3), "-y"), ((2, 1), (1, 1), "+y"))
REST = 64


def moved(place, way):
    return ((place[0] + WAYS[way][0]) % 4, (place[1] + WAYS[way][1]) % 4)


def pairs_of(way):
    dx, dy = WAYS[way]
    return [(y * 4 + x, (y + dy) % 4 * 4 + (x + dx) % 4) for y in range(4) for x in range(4)]


def source_of(place):
    me = lax.axis_index("mp")
    return lax.rem(me // 4 + 4 - place[1], 4) * 4 + lax.rem(lax.rem(me, 4) + 4 - place[0], 4)


def bytes_of(mixed):
    mixed = jnp.bitwise_xor(mixed, jnp.right_shift(mixed, 15))
    mixed = mixed * 1664525 + 1013904223
    mixed = jnp.bitwise_xor(mixed, jnp.right_shift(mixed, 13))
    return jnp.bitwise_and(mixed, 255)


def levels_of(mixed):
    level = bytes_of(mixed).astype(jnp.float32) * (2.0 / 256.0) - 255.0 / 256.0
    return level.astype(jnp.bfloat16)


def iota(shape, dim):
    return lax.broadcasted_iota(jnp.int32, shape, dim)


def by_pair(shape, dim, pairs, seed_ref, first_pair):
    at = iota(shape, dim)
    mixed = lax.rem(at, 4) * CELL_STEP
    for p in range(pairs):
        mixed += jnp.where(at // 4 == p, seed_ref[first_pair + p] * SEED_STEP, 0)
    return mixed


def prepare_kernel(seed_ref, table_ref, gate_ref, up_ref):
    width = gate_ref.shape[1]
    first_pair = lax.axis_index("pop") * 16
    lane = iota((1, 128), 1)
    half = lax.rem(lane, 4) * CELL_STEP + jnp.where(lane >= 64, 33023, 11003)
    for p in range(16):
        half += jnp.where(lax.rem(lane, 64) // 4 == p, seed_ref[first_pair + p] * SEED_STEP, 0)

    @pl.loop(0, table_ref.shape[0] // 32)
    def _(r):
        at = pl.multiple_of(r * 32, 32)
        cell = (iota((32, 128), 0) + at) * (4 * CELL_STEP)
        table_ref[pl.ds(at, 32), :] = levels_of(half + cell)

    first_unit = lax.axis_index("mp") * width
    cell = (iota((16, width), 1) + first_unit) * (4 * CELL_STEP)
    nothing = jnp.zeros((64, width), jnp.bfloat16)
    for i in range(4):
        column = by_pair((16, width), 0, 4, seed_ref, first_pair + 4 * i)
        gate = levels_of(column + cell + 22013)
        up = levels_of(column + cell + 44041)
        for part in (0, 128):
            gate_ref[part + i * 16 : part + i * 16 + 16, :] = gate
            up_ref[part + 64 + i * 16 : part + 64 + i * 16 + 16, :] = up
    for part in (0, 128):
        gate_ref[part + 64 : part + 128, :] = nothing
        up_ref[part : part + 64, :] = nothing


def factor_kernel(seed_ref, message_ref, left_ref, table_ref, lane_ref):
    pairs = seed_ref.shape[0]
    width = table_ref.shape[1] // 2
    count = left_ref.shape[0] // 2
    first = lax.axis_index("mp") * width
    rows = 16
    cell = (iota((rows, width), 1) + first) * (4 * CELL_STEP)

    @pl.loop(0, 4 * pairs // rows)
    def _(i):
        at = pl.multiple_of(i * rows, rows)
        column = by_pair((rows, 128), 0, 4, seed_ref, i * 4)
        mixed = jnp.concatenate([column] * (width // 128), axis=1) + cell
        table_ref[pl.ds(at, rows), :width] = levels_of(mixed + 22013)
        table_ref[pl.ds(at, rows), width:] = levels_of(mixed + 44041)

    left_first = lax.axis_index("pop") * count

    @pl.loop(0, 4 * pairs // 128)
    def _(q):
        lane_ref[...] = jnp.broadcast_to(by_pair((1, 128), 1, 32, seed_ref, q * 32), lane_ref.shape)
        columns = pl.ds(pl.multiple_of(q * 128, 128), 128)

        @pl.loop(0, count // 32)
        def _(i):
            at = pl.multiple_of(i * 32, 32)
            mixed = (iota((32, 128), 0) + (at + left_first)) * (4 * CELL_STEP) + lane_ref[0:1, :]
            left_ref[pl.ds(at, 32), columns] = (bytes_of(mixed + 11003) - 128).astype(jnp.int8)
            left_ref[pl.ds(pl.multiple_of(count + at, 32), 32), columns] = (bytes_of(mixed + 33023) - 128).astype(jnp.int8)


def contract(a, b):
    return lax.dot_general(a, b, (((0,), (0,)), ((), ())), preferred_element_type=jnp.float32)


def product_of(places, blocks, rows, gate_ref, up_ref, table_ref):
    depth = blocks[0].shape[0]
    tokens = jnp.concatenate([block[:, rows] for block in blocks], axis=0)
    weights = []
    for place in places:
        at = pl.ds(pl.multiple_of(source_of(place) * depth, 32), depth)
        weights.append(jnp.concatenate([gate_ref[at, :], up_ref[at, :], table_ref[at, :]], axis=1))
    return contract(tokens, jnp.concatenate(weights, axis=0))


def round_kernel(places, fresh, passed, *refs):
    n = len(places)
    acc_ref, *handed = refs[len(refs) - 1 - len(passed) :]
    for at, out_ref in zip(passed, handed):
        count = out_ref.shape[0]
        first = refs[at].shape[0] - REST if count == REST else 0
        out_ref[...] = refs[at][first : first + count, :]
    tile = 512

    @pl.loop(0, acc_ref.shape[0] // tile)
    def _(i):
        rows = pl.ds(pl.multiple_of(i * tile, tile), tile)
        part = product_of(places, refs[:n], rows, *refs[n : n + 3])
        if fresh:
            acc_ref[rows, :] = part
        else:
            acc_ref[rows, :] = refs[n + 3][rows, :] + part


def last_kernel(pieces, n, depth, *refs):
    blocks, weight_refs = refs[:n], refs[n : n + 3]
    acc_ref, target_ref, weight_ref, gate_out_ref, up_out_ref, message_ref = refs[n + 3 : n + 9]
    total_refs, side_refs, (parts_ref, turned_ref, low_ref) = refs[n + 9 : n + 11], refs[n + 11 : n + 13], refs[n + 13 :]
    width = target_ref.shape[1]
    tile = 256
    tiles = acc_ref.shape[0] // tile
    scale = SIGMA / math.sqrt(16 * depth)
    features = [
        pl.ds(pl.multiple_of(source_of(place) * depth + offset, 16), count) for place, offset, count in pieces
    ]
    lane_pair = lax.rem(iota((tile, 128), 1), 64) // 4
    row_pair = iota((tile, 128), 0) // ROWS

    def weight_columns(low, high):
        gate_ref, up_ref = weight_refs[:2]
        cut = []
        for at in features:
            sides = []
            if low < width:
                sides.append(gate_ref[at, low : min(high, width)])
            if high > width:
                sides.append(up_ref[at, max(low, width) - width : high - width])
            cut.append(sides[0] if len(sides) == 1 else jnp.concatenate(sides, axis=1))
        return jnp.concatenate(cut, axis=0)

    def products(i):
        rows = pl.ds(i * tile, tile)
        total_ref, side_ref = total_refs[i % 2], side_refs[i % 2]

        def turn():
            turned_ref[...] = jnp.concatenate([block[:, rows] for block in blocks], axis=0).T
            table = jnp.concatenate([weight_refs[2][at, :] for at in features], axis=0)
            low = jnp.dot(turned_ref[...], table, preferred_element_type=jnp.float32) + acc_ref[rows, 2 * width :]
            low = jnp.where(lane_pair == row_pair + i * (tile // ROWS), low * scale, 0.0)
            high = low.astype(jnp.bfloat16)
            low_ref[:, :128] = high
            low_ref[:, 128:] = (low - high.astype(jnp.float32)).astype(jnp.bfloat16)

        def side(out_ref, first):
            def step():
                side_ref[:, first : first + width] = jnp.dot(low_ref[...], out_ref[...], preferred_element_type=jnp.float32)

            return step

        def total(low, high):
            def step():
                part = jnp.dot(turned_ref[...], weight_columns(low, high), preferred_element_type=jnp.float32)
                total_ref[:, low:high] = part + acc_ref[rows, low:high]

            return step

        return [turn, side(gate_out_ref, 0), side(up_out_ref, width)] + [
            total(low, low + 256) for low in range(0, 2 * width, 256)
        ]

    def errors(i):
        total_ref, side_ref = total_refs[i % 2], side_refs[i % 2]

        def of_pair(p, kept):
            k = i * (tile // ROWS) + p

            def of_rows(q):
                plus, minus = kept.get(p) or (jnp.zeros((8, width), jnp.float32), jnp.zeros((8, width), jnp.float32))
                at = p * ROWS + q * 16
                goals = target_ref[i * tile + at : i * tile + at + 16, :].astype(jnp.float32)
                for h in range(2):
                    here = slice(at + h * 8, at + h * 8 + 8)
                    goal = goals[h * 8 : h * 8 + 8, :]
                    gate, up = total_ref[here, :width], total_ref[here, width:]
                    side_gate, side_up = side_ref[here, :width], side_ref[here, width:]
                    half = 0.5 * (gate + side_gate)
                    error = (half * jnp.tanh(half) + half) * (up + side_up) - goal
                    plus += error * error
                    half = 0.5 * (gate - side_gate)
                    error = (half * jnp.tanh(half) + half) * (up - side_up) - goal
                    minus += error * error
                kept[p] = (plus, minus)
                if q == ROWS // 16 - 1:
                    parts_ref[0, k : k + 1, :] = jnp.sum(plus, axis=0, keepdims=True) * weight_ref[...][None, :]
                    parts_ref[1, k : k + 1, :] = jnp.sum(minus, axis=0, keepdims=True) * weight_ref[...][None, :]

            return [lambda q=q: of_rows(q) for q in range(ROWS // 16)]

        kept = {}
        return [step for p in range(tile // ROWS) for step in of_pair(p, kept)]

    for step in products(0):
        step()
    for i in range(tiles):
        ahead = products(i + 1) if i + 1 < tiles else []
        behind = errors(i)
        for at, step in enumerate(behind):
            for other in ahead[at * len(ahead) // len(behind) : (at + 1) * len(ahead) // len(behind)]:
                other()
            step()

    pairs = parts_ref.shape[1]
    lane = iota((pairs, 128), 1)
    pair = iota((pairs, 128), 0)
    line = jnp.zeros((1, 128), jnp.float32)
    for s in range(2):
        sums = jnp.sum(parts_ref[s], axis=1, keepdims=True) * (1.0 / (ROWS * FF))
        line += jnp.sum(jnp.where(lane // 4 == pair + 16 * s, sums, 0.0), axis=0, keepdims=True)
    message_ref[...] = jnp.broadcast_to(line, message_ref.shape)


def update_kernel(message_ref, left_ref, table_ref, out_gate, out_up, fit_ref, f_ref, out_gate_ref, out_up_ref, sems):
    rows, width = out_gate_ref.shape
    count = message_ref.shape[0]
    pick_row, pick = iota((16, count), 0), iota((16, count), 1)
    chosen = pick // 16 == 2 * lax.rem(pick_row, 8) + pick_row // 8
    by_pop = jnp.dot(
        chosen.astype(jnp.float32),
        message_ref[...],
        precision=lax.Precision.HIGHEST,
        preferred_element_type=jnp.float32,
    )
    even, odd = by_pop[:8], by_pop[8:]
    low_lane = iota((8, 128), 1) < 64
    plus = jnp.where(low_lane, even, pltpu.roll(odd, 64, 1))
    minus = jnp.where(low_lane, pltpu.roll(even, 64, 1), odd)
    summed = jnp.concatenate([plus, minus], axis=0)
    scores = -summed
    members = 4.0 * 512.0
    center = jnp.sum(scores) / members
    spread = jnp.sum((scores - center) ** 2) / members
    fitness = (scores - center) / jnp.sqrt(jnp.full((16, 128), spread + EPSILON, jnp.float32))
    f_ref[...] = fitness
    factor = (fitness[:8] - fitness[8:]) * (0.5 / 16.0)
    copies = []
    for k, (out_ref, out) in enumerate(((out_gate_ref, out_gate), (out_up_ref, out_up))):
        highs, rests = [], []
        for q in range(8):
            left = left_ref[k * rows : (k + 1) * rows, q * 128 : (q + 1) * 128]
            level = left.astype(jnp.int32).astype(jnp.float32) * (2.0 / 256.0) + 1.0 / 256.0
            scaled = level * factor[q : q + 1, :]
            high = scaled.astype(jnp.bfloat16)
            highs.append(high)
            rests.append((scaled - high.astype(jnp.float32)).astype(jnp.bfloat16))
        right = table_ref[:, k * width : (k + 1) * width]
        out_ref[...] = jnp.dot(
            jnp.concatenate(highs, axis=1), right, preferred_element_type=jnp.float32
        ) + jnp.dot(jnp.concatenate(rests, axis=1), right, preferred_element_type=jnp.float32)
        copies.append(pltpu.make_async_copy(out_ref, out, sems.at[k]))
        copies[-1].start()
    pop = lax.axis_index("pop")
    mine = pop // 2
    lane, member = iota((128, 128), 0), iota((128, 128), 1)
    at = lane == lax.rem(pop, 2) * 64 + member // 2 * 4
    total = jnp.zeros((1, 128), jnp.float32)
    for s in range(2):
        line = jnp.broadcast_to(f_ref[pl.ds(mine + 8 * s, 1), :], (8, 128))
        select = (at & (lax.rem(member, 2) == s)).astype(jnp.float32)
        total += jnp.dot(line, select, precision=lax.Precision.HIGHEST, preferred_element_type=jnp.float32)[:1]
    fit_ref[...] = total[:, : fit_ref.shape[1]]
    for copy in copies:
        copy.wait()


def params(mib):
    return pltpu.CompilerParams(vmem_limit_bytes=mib * 1024 * 1024)


def cost(flops, size):
    return pl.CostEstimate(flops=flops, bytes_accessed=size, transcendentals=0)


def after(value, other):
    return lax.optimization_barrier((value, other))[0]


def on_device(tokens, target, unit_weight, gate_weight, up_weight, seeds):
    rows_dev, depth = tokens.shape
    model_width, width = gate_weight.shape
    pairs_dev = rows_dev // ROWS
    pair_total = seeds.shape[0]
    device_total = lax.axis_size("pop") * lax.axis_size("mp")
    any_space = pl.BlockSpec(memory_space=pl.ANY)
    in_vmem = pl.BlockSpec(memory_space=pltpu.VMEM)
    bf16, f32 = jnp.bfloat16, jnp.float32

    in_smem = pl.BlockSpec(memory_space=pltpu.SMEM)
    columns = 2 * width + 128

    table, gate_out, up_out = pl.pallas_call(
        prepare_kernel,
        out_shape=[jax.ShapeDtypeStruct((model_width, 128), bf16)] + [jax.ShapeDtypeStruct((256, width), bf16)] * 2,
        in_specs=[in_smem],
        out_specs=[in_vmem] * 3,
        compiler_params=params(6),
        cost_estimate=cost(2_000_000_000, 2_000_000),
        name="prepare",
    )(seeds)
    weights = [gate_weight, up_weight, table]

    def multiply(places, acc, passed):
        given = [blocks[place] for place in places] + weights + ([] if acc is None else [acc])
        outs = [jax.ShapeDtypeStruct((rows_dev, columns), f32)]
        for place in passed:
            whole = {ROUNDS[-1][0][0]: depth - REST, HALVES[0][1]: REST, HALVES[1][1]: REST}
            outs.append(jax.ShapeDtypeStruct((whole.get(place, depth), rows_dev), bf16))
        return pl.pallas_call(
            lambda *refs: round_kernel(places, acc is None, [places.index(place) for place in passed], *refs),
            out_shape=outs,
            in_specs=[in_vmem] * len(given),
            out_specs=[in_vmem] * len(outs),
            input_output_aliases={} if acc is None else {len(given) - 1: 0},
            compiler_params=params(12),
            cost_estimate=cost(2 * rows_dev * len(places) * depth * columns, 4_000_000),
            name="round_of_%d" % len(places),
        )(*given)

    blocks = {(0, 0): tokens.T}
    acc, given = None, {}
    held = [(0, 0)]
    for number, sends in enumerate(ROUNDS):
        fresh = {}
        for place, way in sends:
            block = given.get(place, blocks[place])
            if number == 1:
                block = after(block, gate_out)
            elif number == 2:
                block = after(block, given[PASSED[0][0]])
            fresh[moved(place, way)] = lax.ppermute(block, "mp", pairs_of(way))
        if number > 0:
            passed = PASSED[number - 1]
            acc, *handed = multiply(held, acc, passed)
            given.update(zip(passed, handed))
            held = []
        held += list(fresh)
        blocks.update(fresh)

    half = depth // 2
    last = [blocks[place] for place in held]
    pieces = [(place, 0, depth - REST) for place in held]
    for k, (place, other, way) in enumerate(HALVES):
        both = [blocks[place][k * half : (k + 1) * half], given[other]]
        last.append(lax.ppermute(jnp.concatenate(both, axis=0), "mp", pairs_of(way)))
        pieces += [(moved(place, way), k * half, half), (moved(other, way), depth - REST, REST)]
    message = pl.pallas_call(
        lambda *refs: last_kernel(pieces, len(last), depth, *refs),
        out_shape=jax.ShapeDtypeStruct((device_total, 128), f32),
        in_specs=[in_vmem] * (len(last) + 8),
        out_specs=in_vmem,
        scratch_shapes=[pltpu.VMEM((256, 2 * width), f32)] * 4
        + [
            pltpu.VMEM((2, pairs_dev, width), f32),
            pltpu.VMEM((256, sum(block.shape[0] for block in last)), bf16),
            pltpu.VMEM((256, 256), bf16),
        ],
        compiler_params=params(16),
        cost_estimate=cost(2 * rows_dev * 3 * depth * columns, 12_000_000),
        name="last_round",
    )(*last, *weights, acc, target, unit_weight, gate_out, up_out)

    received = lax.all_to_all(message, ("pop", "mp"), 0, 0, tiled=True)

    left_rows = model_width // lax.axis_size("pop")
    left, right = pl.pallas_call(
        factor_kernel,
        out_shape=[
            jax.ShapeDtypeStruct((2 * left_rows, 4 * pair_total), jnp.int8),
            jax.ShapeDtypeStruct((4 * pair_total, 2 * width), bf16),
        ],
        in_specs=[in_smem, any_space],
        out_specs=[in_vmem] * 2,
        scratch_shapes=[pltpu.VMEM((8, 128), jnp.int32)],
        compiler_params=params(8),
        cost_estimate=cost(3_000_000_000, 4_000_000),
        name="factor_tables",
    )(seeds, message)
    update = jax.ShapeDtypeStruct((left_rows, width), f32)
    update_gate, update_up, fitness = pl.pallas_call(
        update_kernel,
        out_shape=[update, update, jax.ShapeDtypeStruct((1, 2 * pairs_dev), f32)],
        in_specs=[in_vmem] * 3,
        out_specs=[any_space, any_space, in_vmem],
        scratch_shapes=[
            pltpu.VMEM((16, 128), f32),
            pltpu.VMEM(update.shape, f32),
            pltpu.VMEM(update.shape, f32),
            pltpu.SemaphoreType.DMA((2,)),
        ],
        compiler_params=params(16),
        cost_estimate=cost(1_200_000_000, 5_000_000),
        name="update",
    )(received, left, right)
    return (update_gate, update_up, fitness.reshape(2 * pairs_dev))


def solution(mesh):
    return jax.shard_map(
        on_device,
        mesh=mesh,
        in_specs=(P("pop", "mp"), P("pop", "mp"), P("mp"), P(None, "mp"), P(None, "mp"), P()),
        out_specs=(P("pop", "mp"), P("pop", "mp"), P("pop")),
        check_vma=False,
    )
```

```python
import math

import jax
import jax.numpy as jnp
from jax import lax
from jax.experimental import pallas as pl
from jax.experimental.pallas import tpu as pltpu
from jax.sharding import PartitionSpec as P

FF = 10240
ROWS = 64
SIGMA = 0.5
EPSILON = 1e-05
SEED_STEP = 747796405
CELL_STEP = 277803737

PASSED = (((0, 1),), ((0, 2), (3, 3), (1, 1)), ())
WAYS = {"+x": (1, 0), "-x": (3, 0), "+y": (0, 1), "-y": (0, 3)}
ROUNDS = (
    (((0, 0), "+x"), ((0, 0), "-y"), ((0, 0), "-x"), ((0, 0), "+y")),
    (((1, 0), "+x"), ((0, 3), "-y"), ((0, 3), "-x"), ((1, 0), "+y")),
    (((0, 3), "+x"), ((2, 0), "-y"), ((0, 1), "-x"), ((2, 0), "+y")),
    (((0, 2), "+x"), ((0, 2), "-x")),
)
HALVES = (((2, 3), (3, 3), "-y"), ((2, 1), (1, 1), "+y"))
REST = 64


def moved(place, way):
    return ((place[0] + WAYS[way][0]) % 4, (place[1] + WAYS[way][1]) % 4)


def pairs_of(way):
    dx, dy = WAYS[way]
    return [(y * 4 + x, (y + dy) % 4 * 4 + (x + dx) % 4) for y in range(4) for x in range(4)]


def source_of(place):
    me = lax.axis_index("mp")
    return lax.rem(me // 4 + 4 - place[1], 4) * 4 + lax.rem(lax.rem(me, 4) + 4 - place[0], 4)


def bytes_of(mixed):
    mixed = jnp.bitwise_xor(mixed, jnp.right_shift(mixed, 15))
    mixed = mixed * 1664525 + 1013904223
    mixed = jnp.bitwise_xor(mixed, jnp.right_shift(mixed, 13))
    return jnp.bitwise_and(mixed, 255)


def levels_of(mixed):
    level = bytes_of(mixed).astype(jnp.float32) * (2.0 / 256.0) - 255.0 / 256.0
    return level.astype(jnp.bfloat16)


def iota(shape, dim):
    return lax.broadcasted_iota(jnp.int32, shape, dim)


def by_pair(shape, dim, pairs, seed_ref, first_pair):
    at = iota(shape, dim)
    mixed = lax.rem(at, 4) * CELL_STEP
    for p in range(pairs):
        mixed += jnp.where(at // 4 == p, seed_ref[first_pair + p] * SEED_STEP, 0)
    return mixed


def prepare_kernel(seed_ref, table_ref, gate_ref, up_ref):
    width = gate_ref.shape[1]
    first_pair = lax.axis_index("pop") * 16
    lane = iota((1, 128), 1)
    half = lax.rem(lane, 4) * CELL_STEP + jnp.where(lane >= 64, 33023, 11003)
    for p in range(16):
        half += jnp.where(lax.rem(lane, 64) // 4 == p, seed_ref[first_pair + p] * SEED_STEP, 0)

    @pl.loop(0, table_ref.shape[0] // 32)
    def _(r):
        at = pl.multiple_of(r * 32, 32)
        cell = (iota((32, 128), 0) + at) * (4 * CELL_STEP)
        table_ref[pl.ds(at, 32), :] = levels_of(half + cell)

    first_unit = lax.axis_index("mp") * width
    cell = (iota((16, width), 1) + first_unit) * (4 * CELL_STEP)
    nothing = jnp.zeros((64, width), jnp.bfloat16)
    for i in range(4):
        column = by_pair((16, width), 0, 4, seed_ref, first_pair + 4 * i)
        gate = levels_of(column + cell + 22013)
        up = levels_of(column + cell + 44041)
        for part in (0, 128):
            gate_ref[part + i * 16 : part + i * 16 + 16, :] = gate
            up_ref[part + 64 + i * 16 : part + 64 + i * 16 + 16, :] = up
    for part in (0, 128):
        gate_ref[part + 64 : part + 128, :] = nothing
        up_ref[part : part + 64, :] = nothing


def factor_kernel(seed_ref, message_ref, left_ref, table_ref, lane_ref):
    pairs = seed_ref.shape[0]
    width = table_ref.shape[1] // 2
    count = left_ref.shape[0] // 2
    first = lax.axis_index("mp") * width
    rows = 16
    cell = (iota((rows, width), 1) + first) * (4 * CELL_STEP)

    @pl.loop(0, 4 * pairs // rows)
    def _(i):
        at = pl.multiple_of(i * rows, rows)
        column = by_pair((rows, 128), 0, 4, seed_ref, i * 4)
        mixed = jnp.concatenate([column] * (width // 128), axis=1) + cell
        table_ref[pl.ds(at, rows), :width] = levels_of(mixed + 22013)
        table_ref[pl.ds(at, rows), width:] = levels_of(mixed + 44041)

    left_first = lax.axis_index("pop") * count

    @pl.loop(0, 4 * pairs // 128)
    def _(q):
        lane_ref[...] = jnp.broadcast_to(by_pair((1, 128), 1, 32, seed_ref, q * 32), lane_ref.shape)
        columns = pl.ds(pl.multiple_of(q * 128, 128), 128)

        @pl.loop(0, count // 32)
        def _(i):
            at = pl.multiple_of(i * 32, 32)
            mixed = (iota((32, 128), 0) + (at + left_first)) * (4 * CELL_STEP) + lane_ref[0:1, :]
            left_ref[pl.ds(at, 32), columns] = (bytes_of(mixed + 11003) - 128).astype(jnp.int8)
            left_ref[pl.ds(pl.multiple_of(count + at, 32), 32), columns] = (bytes_of(mixed + 33023) - 128).astype(jnp.int8)


def contract(a, b):
    return lax.dot_general(a, b, (((0,), (0,)), ((), ())), preferred_element_type=jnp.float32)


def product_of(places, blocks, rows, gate_ref, up_ref, table_ref):
    depth = blocks[0].shape[0]
    tokens = jnp.concatenate([block[:, rows] for block in blocks], axis=0)
    weights = []
    for place in places:
        at = pl.ds(pl.multiple_of(source_of(place) * depth, 32), depth)
        weights.append(jnp.concatenate([gate_ref[at, :], up_ref[at, :], table_ref[at, :]], axis=1))
    return contract(tokens, jnp.concatenate(weights, axis=0))


def round_kernel(places, fresh, passed, *refs):
    n = len(places)
    acc_ref, *handed = refs[len(refs) - 1 - len(passed) :]
    for at, out_ref in zip(passed, handed):
        count = out_ref.shape[0]
        first = refs[at].shape[0] - REST if count == REST else 0
        out_ref[...] = refs[at][first : first + count, :]
    tile = 1024

    @pl.loop(0, acc_ref.shape[0] // tile)
    def _(i):
        rows = pl.ds(pl.multiple_of(i * tile, tile), tile)
        part = product_of(places, refs[:n], rows, *refs[n : n + 3])
        if fresh:
            acc_ref[rows, :] = part
        else:
            acc_ref[rows, :] = refs[n + 3][rows, :] + part


def last_kernel(pieces, n, depth, *refs):
    blocks, weight_refs = refs[:n], refs[n : n + 3]
    acc_ref, target_ref, weight_ref, gate_out_ref, up_out_ref, message_ref = refs[n + 3 : n + 9]
    total_refs, side_refs, (parts_ref, turned_ref, low_ref) = refs[n + 9 : n + 11], refs[n + 11 : n + 13], refs[n + 13 :]
    width = target_ref.shape[1]
    tile = 256
    tiles = acc_ref.shape[0] // tile
    scale = SIGMA / math.sqrt(16 * depth)
    features = [
        pl.ds(pl.multiple_of(source_of(place) * depth + offset, 16), count) for place, offset, count in pieces
    ]
    lane_pair = lax.rem(iota((tile, 128), 1), 64) // 4
    row_pair = iota((tile, 128), 0) // ROWS

    def weight_columns(low, high):
        gate_ref, up_ref = weight_refs[:2]
        cut = []
        for at in features:
            sides = []
            if low < width:
                sides.append(gate_ref[at, low : min(high, width)])
            if high > width:
                sides.append(up_ref[at, max(low, width) - width : high - width])
            cut.append(sides[0] if len(sides) == 1 else jnp.concatenate(sides, axis=1))
        return jnp.concatenate(cut, axis=0)

    def products(i):
        rows = pl.ds(i * tile, tile)
        total_ref, side_ref = total_refs[i % 2], side_refs[i % 2]

        def turn():
            turned_ref[...] = jnp.concatenate([block[:, rows] for block in blocks], axis=0).T
            table = jnp.concatenate([weight_refs[2][at, :] for at in features], axis=0)
            low = jnp.dot(turned_ref[...], table, preferred_element_type=jnp.float32) + acc_ref[rows, 2 * width :]
            low = jnp.where(lane_pair == row_pair + i * (tile // ROWS), low * scale, 0.0)
            high = low.astype(jnp.bfloat16)
            low_ref[:, :128] = high
            low_ref[:, 128:] = (low - high.astype(jnp.float32)).astype(jnp.bfloat16)

        def side(out_ref, first):
            def step():
                side_ref[:, first : first + width] = jnp.dot(low_ref[...], out_ref[...], preferred_element_type=jnp.float32)

            return step

        def total(low, high):
            def step():
                part = jnp.dot(turned_ref[...], weight_columns(low, high), preferred_element_type=jnp.float32)
                total_ref[:, low:high] = part + acc_ref[rows, low:high]

            return step

        return [turn, side(gate_out_ref, 0), side(up_out_ref, width)] + [
            total(low, low + 256) for low in range(0, 2 * width, 256)
        ]

    def errors(i):
        total_ref, side_ref = total_refs[i % 2], side_refs[i % 2]

        def of_pair(p, kept):
            k = i * (tile // ROWS) + p

            def of_rows(q):
                plus, minus = kept.get(p) or (jnp.zeros((8, width), jnp.float32), jnp.zeros((8, width), jnp.float32))
                at = p * ROWS + q * 16
                goals = target_ref[i * tile + at : i * tile + at + 16, :].astype(jnp.float32)
                for h in range(2):
                    here = slice(at + h * 8, at + h * 8 + 8)
                    goal = goals[h * 8 : h * 8 + 8, :]
                    gate, up = total_ref[here, :width], total_ref[here, width:]
                    side_gate, side_up = side_ref[here, :width], side_ref[here, width:]
                    half = 0.5 * (gate + side_gate)
                    error = (half * jnp.tanh(half) + half) * (up + side_up) - goal
                    plus += error * error
                    half = 0.5 * (gate - side_gate)
                    error = (half * jnp.tanh(half) + half) * (up - side_up) - goal
                    minus += error * error
                kept[p] = (plus, minus)
                if q == ROWS // 16 - 1:
                    parts_ref[0, k : k + 1, :] = jnp.sum(plus, axis=0, keepdims=True) * weight_ref[...][None, :]
                    parts_ref[1, k : k + 1, :] = jnp.sum(minus, axis=0, keepdims=True) * weight_ref[...][None, :]

            return [lambda q=q: of_rows(q) for q in range(ROWS // 16)]

        kept = {}
        return [step for p in range(tile // ROWS) for step in of_pair(p, kept)]

    for step in products(0):
        step()
    for i in range(tiles):
        ahead = products(i + 1) if i + 1 < tiles else []
        behind = errors(i)
        for at, step in enumerate(behind):
            for other in ahead[at * len(ahead) // len(behind) : (at + 1) * len(ahead) // len(behind)]:
                other()
            step()

    pairs = parts_ref.shape[1]
    lane = iota((pairs, 128), 1)
    pair = iota((pairs, 128), 0)
    line = jnp.zeros((1, 128), jnp.float32)
    for s in range(2):
        sums = jnp.sum(parts_ref[s], axis=1, keepdims=True) * (1.0 / (ROWS * FF))
        line += jnp.sum(jnp.where(lane // 4 == pair + 16 * s, sums, 0.0), axis=0, keepdims=True)
    message_ref[...] = jnp.broadcast_to(line, message_ref.shape)


def update_kernel(message_ref, left_ref, table_ref, out_gate, out_up, fit_ref, f_ref, out_gate_ref, out_up_ref, sems):
    rows, width = out_gate_ref.shape
    count = message_ref.shape[0]
    pick_row, pick = iota((16, count), 0), iota((16, count), 1)
    chosen = pick // 16 == 2 * lax.rem(pick_row, 8) + pick_row // 8
    by_pop = jnp.dot(
        chosen.astype(jnp.float32),
        message_ref[...],
        precision=lax.Precision.HIGHEST,
        preferred_element_type=jnp.float32,
    )
    even, odd = by_pop[:8], by_pop[8:]
    low_lane = iota((8, 128), 1) < 64
    plus = jnp.where(low_lane, even, pltpu.roll(odd, 64, 1))
    minus = jnp.where(low_lane, pltpu.roll(even, 64, 1), odd)
    summed = jnp.concatenate([plus, minus], axis=0)
    scores = -summed
    members = 4.0 * 512.0
    center = jnp.sum(scores) / members
    spread = jnp.sum((scores - center) ** 2) / members
    fitness = (scores - center) / jnp.sqrt(jnp.full((16, 128), spread + EPSILON, jnp.float32))
    f_ref[...] = fitness
    factor = (fitness[:8] - fitness[8:]) * (0.5 / 16.0)
    pop = lax.axis_index("pop")
    mine = pop // 2
    lane, member = iota((128, 128), 0), iota((128, 128), 1)
    at = lane == lax.rem(pop, 2) * 64 + member // 2 * 4
    total = jnp.zeros((1, 128), jnp.float32)
    for s in range(2):
        line = jnp.broadcast_to(f_ref[pl.ds(mine + 8 * s, 1), :], (8, 128))
        select = (at & (lax.rem(member, 2) == s)).astype(jnp.float32)
        total += jnp.dot(line, select, precision=lax.Precision.HIGHEST, preferred_element_type=jnp.float32)[:1]
    fit_ref[...] = total[:, : fit_ref.shape[1]]
    copies = []
    for k, (out_ref, out) in enumerate(((out_gate_ref, out_gate), (out_up_ref, out_up))):
        highs, rests = [], []
        for q in range(8):
            left = left_ref[k * rows : (k + 1) * rows, q * 128 : (q + 1) * 128]
            level = left.astype(jnp.int32).astype(jnp.float32) * (2.0 / 256.0) + 1.0 / 256.0
            scaled = level * factor[q : q + 1, :]
            high = scaled.astype(jnp.bfloat16)
            highs.append(high)
            rests.append((scaled - high.astype(jnp.float32)).astype(jnp.bfloat16))
        right = table_ref[:, k * width : (k + 1) * width]
        out_ref[...] = jnp.dot(
            jnp.concatenate(highs, axis=1), right, preferred_element_type=jnp.float32
        ) + jnp.dot(jnp.concatenate(rests, axis=1), right, preferred_element_type=jnp.float32)
        copies.append(pltpu.make_async_copy(out_ref, out, sems.at[k]))
        copies[-1].start()
    for copy in copies:
        copy.wait()


def params(mib):
    return pltpu.CompilerParams(vmem_limit_bytes=mib * 1024 * 1024)


def cost(flops, size):
    return pl.CostEstimate(flops=flops, bytes_accessed=size, transcendentals=0)


def after(value, other):
    return lax.optimization_barrier((value, other))[0]


def on_device(tokens, target, unit_weight, gate_weight, up_weight, seeds):
    rows_dev, depth = tokens.shape
    model_width, width = gate_weight.shape
    pairs_dev = rows_dev // ROWS
    pair_total = seeds.shape[0]
    device_total = lax.axis_size("pop") * lax.axis_size("mp")
    any_space = pl.BlockSpec(memory_space=pl.ANY)
    in_vmem = pl.BlockSpec(memory_space=pltpu.VMEM)
    bf16, f32 = jnp.bfloat16, jnp.float32

    in_smem = pl.BlockSpec(memory_space=pltpu.SMEM)
    columns = 2 * width + 128

    table, gate_out, up_out = pl.pallas_call(
        prepare_kernel,
        out_shape=[jax.ShapeDtypeStruct((model_width, 128), bf16)] + [jax.ShapeDtypeStruct((256, width), bf16)] * 2,
        in_specs=[in_smem],
        out_specs=[in_vmem] * 3,
        compiler_params=params(6),
        cost_estimate=cost(2_000_000_000, 2_000_000),
        name="prepare",
    )(seeds)
    weights = [gate_weight, up_weight, table]

    def multiply(places, acc, passed):
        given = [blocks[place] for place in places] + weights + ([] if acc is None else [acc])
        outs = [jax.ShapeDtypeStruct((rows_dev, columns), f32)]
        for place in passed:
            whole = {ROUNDS[-1][0][0]: depth - REST, HALVES[0][1]: REST, HALVES[1][1]: REST}
            outs.append(jax.ShapeDtypeStruct((whole.get(place, depth), rows_dev), bf16))
        return pl.pallas_call(
            lambda *refs: round_kernel(places, acc is None, [places.index(place) for place in passed], *refs),
            out_shape=outs,
            in_specs=[in_vmem] * len(given),
            out_specs=[in_vmem] * len(outs),
            input_output_aliases={} if acc is None else {len(given) - 1: 0},
            compiler_params=params(12),
            cost_estimate=cost(2 * rows_dev * len(places) * depth * columns, 4_000_000),
            name="round_of_%d" % len(places),
        )(*given)

    blocks = {(0, 0): tokens.T}
    acc, given = None, {}
    held = [(0, 0)]
    for number, sends in enumerate(ROUNDS):
        fresh = {}
        for place, way in sends:
            block = given.get(place, blocks[place])
            if number == 1:
                block = after(block, gate_out)
            elif number == 2:
                block = after(block, given[PASSED[0][0]])
            fresh[moved(place, way)] = lax.ppermute(block, "mp", pairs_of(way))
        if number > 0:
            passed = PASSED[number - 1]
            acc, *handed = multiply(held, acc, passed)
            given.update(zip(passed, handed))
            held = []
        held += list(fresh)
        blocks.update(fresh)

    half = depth // 2
    last = [blocks[place] for place in held]
    pieces = [(place, 0, depth - REST) for place in held]
    for k, (place, other, way) in enumerate(HALVES):
        both = [blocks[place][k * half : (k + 1) * half], given[other]]
        last.append(lax.ppermute(jnp.concatenate(both, axis=0), "mp", pairs_of(way)))
        pieces += [(moved(place, way), k * half, half), (moved(other, way), depth - REST, REST)]
    message = pl.pallas_call(
        lambda *refs: last_kernel(pieces, len(last), depth, *refs),
        out_shape=jax.ShapeDtypeStruct((device_total, 128), f32),
        in_specs=[in_vmem] * (len(last) + 8),
        out_specs=in_vmem,
        scratch_shapes=[pltpu.VMEM((256, 2 * width), f32)] * 4
        + [
            pltpu.VMEM((2, pairs_dev, width), f32),
            pltpu.VMEM((256, sum(block.shape[0] for block in last)), bf16),
            pltpu.VMEM((256, 256), bf16),
        ],
        compiler_params=params(16),
        cost_estimate=cost(2 * rows_dev * 3 * depth * columns, 12_000_000),
        name="last_round",
    )(*last, *weights, acc, target, unit_weight, gate_out, up_out)

    received = lax.all_to_all(message, ("pop", "mp"), 0, 0, tiled=True)

    left_rows = model_width // lax.axis_size("pop")
    left, right = pl.pallas_call(
        factor_kernel,
        out_shape=[
            jax.ShapeDtypeStruct((2 * left_rows, 4 * pair_total), jnp.int8),
            jax.ShapeDtypeStruct((4 * pair_total, 2 * width), bf16),
        ],
        in_specs=[in_smem, any_space],
        out_specs=[in_vmem] * 2,
        scratch_shapes=[pltpu.VMEM((8, 128), jnp.int32)],
        compiler_params=params(8),
        cost_estimate=cost(3_000_000_000, 4_000_000),
        name="factor_tables",
    )(seeds, message)
    update = jax.ShapeDtypeStruct((left_rows, width), f32)
    update_gate, update_up, fitness = pl.pallas_call(
        update_kernel,
        out_shape=[update, update, jax.ShapeDtypeStruct((1, 2 * pairs_dev), f32)],
        in_specs=[in_vmem] * 3,
        out_specs=[any_space, any_space, in_vmem],
        scratch_shapes=[
            pltpu.VMEM((16, 128), f32),
            pltpu.VMEM(update.shape, f32),
            pltpu.VMEM(update.shape, f32),
            pltpu.SemaphoreType.DMA((2,)),
        ],
        compiler_params=params(16),
        cost_estimate=cost(1_200_000_000, 5_000_000),
        name="update",
    )(received, left, right)
    return (update_gate, update_up, fitness.reshape(2 * pairs_dev))


def solution(mesh):
    return jax.shard_map(
        on_device,
        mesh=mesh,
        in_specs=(P("pop", "mp"), P("pop", "mp"), P("mp"), P(None, "mp"), P(None, "mp"), P()),
        out_specs=(P("pop", "mp"), P("pop", "mp"), P("pop")),
        check_vma=False,
    )
```
